32 devices in a mesh: row: 4 (over z), col: 8 (over y, x, core).
Axes of the slice: x: 2, y: 2, z: 4, core: 2. Of those that a mesh axis runs over, the one named last changes fastest.
Arguments:
- ingest_features: bfloat16 [8192, 1536], P(('row', 'col')), may hold values from -40 to 40
- node_map: int32 [8192], P(('row', 'col')), may hold values from 0 to 4095, as said below
- unit_rows: int32 [32], P(('row', 'col')), may hold values from 0 to 256, as said below
- tile_ids: int32 [768, 2], P(('row', 'col')), may hold values from 0 to 32, as said below
- tile_values: bfloat16 [768, 128, 128], P(('row', 'col')), may hold values from -40 to 40
- mix_in: bfloat16 [128, 128], replicated, may hold values from -0.5 to 0.5
- mix_out: bfloat16 [128, 128], replicated, may hold values from -0.5 to 0.5
Outputs:
- residual: float32 [4096, 1536], P(('row', 'col'))
The draws below stay inside these ranges and needn't reach their ends.
Inputs may be any that keep to these rules, and one draw needn't show every extreme that they name: `node_map`: for every unit u the first unit_rows[u] of its 256 slots name distinct nodes, and all units' such slots together name every node exactly once; at most 8 of them of one unit name nodes of one partition (nodes k * 128 to (k + 1) * 128 - 1), and one unit names exactly 8 in every partition. Entries of the other slots are arbitrary nodes. `unit_rows`: one unit delivers 256 rows. `tile_ids`: slots k * 24 to (k + 1) * 24 - 1 hold first some distinct tiles whose row tile lies in row block k // 8 (tile rows (8 times that) onward) and whose column tile lies in column block k % 8, then padding slots whose row tile and column tile are both 4096 // 128. Some blocks have no padding slot.
All inputs are finite; a program needn't handle non-finite values.
Results may differ from the reference program's by a relative error of at most 0.0095.
Values may be sent and summed in bfloat16 or wider, within the bound.
No kernel may reach another device: no remote copies, remote signals or barrier semaphores. Data moves between devices by JAX's collectives and lax.ppermute only.
A program may use at most 64 MiB of HBM per device.

```python
import jax
import jax.numpy as jnp
from jax import lax

CH = 128
TILE = 128
PIECE = 128
FEAT = 1536
ROW_GROUPS = 4
COL_GROUPS = 8
INGEST_PARTS = 32
NODES = 4096
ROW_TILES = 8
COL_TILES = 4
TILES_DEV = 24
SLOTS = 768
PAIR = 8
CAP = 256
N_ROW = 4
N_COL = 8


def ingest_tables(key):
    selection_key, extra_random_key, weighty_random_key, ordering_random_key, padding_random_key = jax.random.split(key, 5)
    total_slot_count = INGEST_PARTS * PAIR
    owning_partition = jnp.arange(total_slot_count, dtype=jnp.int32) // PAIR
    extra_amount = jax.random.randint(extra_random_key, (INGEST_PARTS,), 0, 256)
    heavy = jax.random.randint(weighty_random_key, (), 0, INGEST_PARTS)
    base_amount = jax.random.randint(selection_key, (INGEST_PARTS, total_slot_count), 0, 1024) + 4 * extra_amount[owning_partition][None, :]
    base_amount = jnp.where((owning_partition == heavy)[None, :], -4096, base_amount)
    score = base_amount * total_slot_count + jnp.arange(total_slot_count, dtype=jnp.int32)[None, :]
    unused, chosen = lax.top_k(-score, PIECE)
    partition = jnp.arange(INGEST_PARTS, dtype=jnp.int32)[:, None]
    placed = partition * PIECE + jnp.arange(PIECE, dtype=jnp.int32)[None, :]
    node_at = jnp.full((INGEST_PARTS, total_slot_count), -1, jnp.int32).at[partition, chosen].set(placed)
    candidates = node_at.reshape(INGEST_PARTS, INGEST_PARTS, PAIR).transpose(1, 0, 2).reshape(INGEST_PARTS, CAP)
    alive = (candidates >= 0).astype(jnp.int32)
    shuffle = jax.random.randint(ordering_random_key, (INGEST_PARTS, CAP), 0, 4096)
    order_score = (1 - alive) * (1 << 25) + shuffle * CAP + jnp.arange(CAP, dtype=jnp.int32)[None, :]
    order = jnp.argsort(order_score, axis=1, stable=True)
    arranged = jnp.take_along_axis(candidates, order, axis=1)
    counts = jnp.sum(alive, axis=1).astype(jnp.int32)
    filler = jax.random.randint(padding_random_key, (INGEST_PARTS, CAP), 0, NODES)
    mapping = jnp.where(arranged >= 0, arranged, filler).reshape(-1).astype(jnp.int32)
    return (mapping, counts)


def draw_node_map(key, part):
    return ingest_tables(jax.random.fold_in(key, 5))[0]


def draw_unit_rows(key, part):
    return ingest_tables(jax.random.fold_in(key, 5))[1]


def tile_layout(key):

    def one_device(device):
        row_block = device // COL_GROUPS
        col_block = device % COL_GROUPS
        near = (col_block * N_ROW < (row_block + 1) * N_COL) & (row_block * N_COL < (col_block + 1) * N_ROW)
        few = jax.random.randint(jax.random.fold_in(key, device + 7919), (), TILES_DEV // 8, TILES_DEV // 4 + 1)
        count = jnp.where(near, TILES_DEV, few)
        order = jax.random.permutation(jax.random.fold_in(key, device), ROW_TILES * COL_TILES)[:TILES_DEV]
        row_tile = order // COL_TILES + row_block * ROW_TILES
        col_tile = order % COL_TILES + col_block * COL_TILES
        real = jnp.arange(TILES_DEV, dtype=jnp.int32) < count
        pad = NODES // TILE
        row_tile = jnp.where(real, row_tile, pad)
        col_tile = jnp.where(real, col_tile, pad)
        return jnp.stack([row_tile, col_tile], axis=-1).astype(jnp.int32)
    return jax.vmap(one_device)(jnp.arange(INGEST_PARTS, dtype=jnp.int32)).reshape(SLOTS, 2)


def draw_tile_ids(key, part):
    return tile_layout(jax.random.fold_in(key, 11))


def draw_tile_values(key, part):
    layout = jnp.minimum(tile_layout(jax.random.fold_in(key, 11)), NODES // TILE - 1)
    row_key, col_key, entry_key = jax.random.split(jax.random.fold_in(key, 12), 3)
    low = jnp.log(0.3)
    high = jnp.log(3.0)
    row_scale = jnp.exp(jax.random.uniform(row_key, (NODES,), jnp.float32, low, high))
    col_scale = jnp.exp(jax.random.uniform(col_key, (NODES,), jnp.float32, low, high))
    inside = jnp.arange(TILE, dtype=jnp.int32)[None, :]
    row_part = row_scale[layout[:, 0:1] * TILE + inside]
    col_part = col_scale[layout[:, 1:2] * TILE + inside]
    entries = jnp.clip(jax.random.normal(entry_key, (SLOTS, TILE, TILE), jnp.float32), -4.0, 4.0)
    return (entries * row_part[:, :, None] * col_part[:, None, :]).astype(jnp.bfloat16)


def draw_ingest_features(key, part):
    slot_key, column_key, entry_key = jax.random.split(key, 3)
    low = jnp.log(0.3)
    high = jnp.log(3.0)
    slot_scale = jnp.exp(jax.random.uniform(slot_key, (INGEST_PARTS * CAP, 1), jnp.float32, low, high))
    column_scale = jnp.exp(jax.random.uniform(column_key, (1, FEAT), jnp.float32, low, high))
    entries = jnp.clip(jax.random.normal(entry_key, (INGEST_PARTS * CAP, FEAT), jnp.float32), -4.0, 4.0)
    return (entries * slot_scale * column_scale).astype(jnp.bfloat16)


def scatter_about(stream_key, dims, scale, reach, kind=jnp.bfloat16):
    values = jax.random.normal(stream_key, dims, jnp.float32) * scale
    return jnp.minimum(jnp.maximum(values, -reach), reach).astype(kind)


def setup_inputs(seed: int = 0) -> dict:
    key_list = jax.random.split(jax.random.key(seed), 8)
    return {
        "ingest_features": draw_ingest_features(jax.random.fold_in(key_list[7], 71), 0),
        "node_map": draw_node_map(jax.random.fold_in(key_list[7], 71), 0),
        "unit_rows": draw_unit_rows(jax.random.fold_in(key_list[7], 71), 0),
        "tile_ids": draw_tile_ids(jax.random.fold_in(key_list[7], 71), 0),
        "tile_values": draw_tile_values(jax.random.fold_in(key_list[7], 71), 0),
        "mix_in": scatter_about(key_list[5], (CH, CH), CH ** -0.5, 0.5),
        "mix_out": scatter_about(key_list[6], (CH, CH), CH ** -0.5, 0.5),
    }


epsilon = 1e-05

def normalize(values):
    groups = values.reshape(-1, CH)
    power = lax.optimization_barrier(jnp.mean(groups * groups, axis=-1, keepdims=True))
    return (groups * lax.rsqrt(power + epsilon)).astype(jnp.bfloat16)

def encode(totals, mix_in):
    row_total = totals.shape[0]
    mixed = jnp.dot(normalize(totals), mix_in, preferred_element_type=jnp.float32)
    return jax.nn.gelu(mixed, approximate=False).astype(jnp.bfloat16).reshape(row_total, -1)

def dense_block(tile_ids, tile_values, row_index, col_index, row_tiles, col_tiles):
    local_rows = tile_ids[:, 0] - row_index * row_tiles
    local_cols = tile_ids[:, 1] - col_index * col_tiles
    tile_edge = tile_values.shape[1]
    tile_grid = jnp.zeros((row_tiles, col_tiles, tile_edge, tile_edge), tile_values.dtype)
    tile_grid = tile_grid.at[local_rows, local_cols].set(tile_values, mode='drop')
    return tile_grid.transpose(0, 2, 1, 3).reshape(row_tiles * tile_edge, col_tiles * tile_edge)

def reference(ingest_features, node_map, unit_rows, tile_ids, tile_values, mix_in, mix_out):
    live = (jnp.arange(CAP, dtype=jnp.int32)[None, :] < unit_rows[:, None]).reshape(-1)
    target = jnp.where(live, node_map, NODES)
    features = jnp.zeros((NODES, FEAT), jnp.bfloat16).at[target].set(ingest_features, mode='drop')
    span_rows = ROW_TILES * TILE
    span_cols = COL_TILES * TILE

    def block_at(row_index, col_index):
        device = row_index * COL_GROUPS + col_index
        chosen_ids = lax.dynamic_slice_in_dim(tile_ids, device * TILES_DEV, TILES_DEV, 0)
        chosen_values = lax.dynamic_slice_in_dim(tile_values, device * TILES_DEV, TILES_DEV, 0)
        return dense_block(chosen_ids, chosen_values, row_index, col_index, ROW_TILES, COL_TILES)

    def back_parts(row_index, panel):

        def one_part(col_index):
            product = lax.dot_general(block_at(row_index, col_index), panel, (((0,), (0,)), ((), ())), preferred_element_type=jnp.float32)
            return product.astype(jnp.bfloat16)
        return lax.map(one_part, jnp.arange(COL_GROUPS, dtype=jnp.int32))
    back_sum = jnp.zeros((NODES, FEAT), jnp.float32)
    for row_index in range(ROW_GROUPS):
        panel = features[row_index * span_rows:(row_index + 1) * span_rows]
        back_sum = back_sum + back_parts(row_index, panel).reshape(NODES, FEAT).astype(jnp.float32)
    hidden = encode(back_sum, mix_in)

    def forward_parts(col_index, panel):

        def one_part(row_index):
            product = jnp.dot(block_at(row_index, col_index), panel, preferred_element_type=jnp.float32)
            return product.astype(jnp.bfloat16)
        return lax.map(one_part, jnp.arange(ROW_GROUPS, dtype=jnp.int32))
    forward_sum = jnp.zeros((NODES, FEAT), jnp.float32)
    for col_index in range(COL_GROUPS):
        panel = hidden[col_index * span_cols:(col_index + 1) * span_cols]
        forward_sum = forward_sum + forward_parts(col_index, panel).reshape(NODES, FEAT).astype(jnp.float32)
    recon = jnp.dot(normalize(forward_sum), mix_out, preferred_element_type=jnp.float32).reshape(NODES, FEAT)
    return features.astype(jnp.float32) - recon
```

```python
import functools

import jax
import jax.numpy as jnp
from jax import lax
from jax.experimental import pallas as pl
from jax.experimental.pallas import tpu as pltpu
from jax.sharding import PartitionSpec as P

CH = 128
TILE = 128
PIECE = 128
QUARTERS = 4
VMEM_LIMIT = 56 * 1024 * 1024

epsilon = 1e-05

BF16 = jnp.bfloat16
F32 = jnp.float32
VM = pl.BlockSpec(memory_space=pltpu.VMEM)
SM = pl.BlockSpec(memory_space=pltpu.SMEM)


def iota(shape, axis):
    return lax.broadcasted_iota(jnp.int32, shape, axis)


def call(kernel, out_shape, in_specs, out_specs=None, flops=0, bytes_accessed=0, **kw):
    many = isinstance(out_shape, (list, tuple))
    if out_specs is None:
        out_specs = [VM] * len(out_shape) if many else VM
    return pl.pallas_call(
        kernel,
        out_shape=out_shape,
        in_specs=in_specs,
        out_specs=out_specs,
        compiler_params=pltpu.CompilerParams(vmem_limit_bytes=VMEM_LIMIT),
        cost_estimate=pl.CostEstimate(
            flops=flops, bytes_accessed=bytes_accessed, transcendentals=0
        ),
        **kw,
    )


class Layout:
    def __init__(self, rows, cols, slots, width):
        self.R, self.C = rows, cols
        self.R2, self.chips = rows // 2, cols // 2
        self.U = rows * cols
        self.slots = slots
        self.pair = slots // self.U
        self.slab = 4 * self.pair
        self.upl = CH // self.slab
        self.groups = width // CH // QUARTERS
        self.qw = self.groups * CH
        self.blocks = self.R2 * self.chips
        self.own = 4 * PIECE
        self.chip_cols = 2 * rows * TILE
        self.tpl = 2 * rows // self.R2
        self.pay = self.groups * self.slab + 8

    def split_z(self, z):
        return z // self.R2, z % self.R2

    def join_z(self, h, l):
        return h * self.R2 + l


def pack_kernel(lay, me, node, feats, out):
    unit, count = me[0], me[1]
    n = lay.slots
    row = node[...]
    slot = iota((1, n), 1)
    live = slot < count
    p = row // PIECE
    h, l = lay.split_z(p // lay.C)
    c = p % lay.C
    block = l * lay.chips + c // 2
    part = h * 2 + c % 2
    p = jnp.where(live, p, -1)
    across = jnp.broadcast_to(p, (n, n))
    down = jnp.transpose(across)
    before = (across == down) & (iota((n, n), 0) < iota((n, n), 1))
    rank = jnp.sum(jnp.where(before, 1, 0), axis=0, keepdims=True)
    target = jnp.where(live, (block * 4 + part) * lay.pair + rank, -1)
    pick = jnp.where(iota((n, n), 0) == target, 1.0, 0.0).astype(BF16)
    sorted_rows = jnp.dot(pick, feats[...], preferred_element_type=F32).astype(BF16)
    place = jnp.where(live, row % PIECE + 1, 0).astype(F32).astype(BF16)
    place = jnp.broadcast_to(place, (16, n))
    lane = iota((lay.blocks * CH, n), 0)
    inner = lane % CH - (unit % lay.upl) * lay.slab
    wanted = (lane // CH) * lay.slab + inner
    wanted = jnp.where((inner >= 0) & (inner < lay.slab), wanted, -2)
    spread = jnp.where(wanted == target, 1.0, 0.0).astype(BF16)
    places = lax.dot_general(
        place, spread, (((1,), (1,)), ((), ())), preferred_element_type=F32
    ).astype(BF16)
    for z in range(lay.R):
        dh, dl = lay.split_z(z)
        for c in range(lay.C):
            b = dl * lay.chips + c // 2
            q = dh * 2 + c % 2
            d = z * lay.C + c
            for g in range(lay.groups):
                lo = q * lay.qw + g * CH
                out[d, g * lay.slab : (g + 1) * lay.slab, :] = sorted_rows[
                    b * lay.slab : (b + 1) * lay.slab, lo : lo + CH
                ]
            out[d, lay.groups * lay.slab : lay.pay, :] = places[0:8, b * CH : (b + 1) * CH]


def land_kernel(lay, chunks, me, got, *outs):
    mine = me[2]
    lane = iota((1, CH), 1)
    part = (lane % lay.slab) // lay.pair
    base = (part ^ mine) * PIECE - 1
    rows = iota((lay.own, CH), 0)
    picks = []
    for j in range(lay.U // lay.upl):
        total = jnp.zeros((8, CH), F32)
        for i in range(lay.upl):
            total = total + got[j * lay.upl + i, lay.groups * lay.slab : lay.pay, :].astype(F32)
        place = total[0:1, :].astype(jnp.int32)
        spot = jnp.where(place > 0, base + place, -1)
        picks.append(jnp.where(rows == spot, 1.0, 0.0).astype(BF16))
    pick = jnp.concatenate(picks, axis=1)
    for out, (first, many) in zip(outs, chunks):
        for g in range(many):
            lo = (first + g) * lay.slab
            block = got[:, lo : lo + lay.slab, :].reshape(lay.U * lay.slab, CH)
            out[:, g * CH : (g + 1) * CH] = jnp.dot(
                pick, block, preferred_element_type=F32
            ).astype(BF16)


def dense_kernel(lay, step_rows, me, i0, i1, i2, i3, v0, v1, v2, v3, a, at):
    h, l, chip, core = me[3], me[4], me[5], me[6]
    first = pl.program_id(0) * step_rows
    a[...] = jnp.zeros_like(a)
    at[...] = jnp.zeros_like(at)
    tiles = step_rows // TILE
    for ids, values in ((i0, v0), (i1, v1), (i2, v2), (i3, v3)):

        def body(t, carry, ids=ids, values=values):
            rt, ct = ids[2 * t], ids[2 * t + 1]
            zh, zl = lay.split_z(rt // lay.C)
            c = rt % lay.C
            r = ((c // 2) ^ chip) * 4 + (zh ^ h) * 2 + ((c % 2) ^ core) - first // TILE
            cc = ct // lay.R
            j = (cc % 2) * lay.R + ct % lay.R
            k = ((j // lay.tpl) ^ l) * lay.tpl + j % lay.tpl

            @pl.when((rt < lay.U) & (r >= 0) & (r < tiles))
            def _():
                rr = pl.multiple_of(r * TILE, TILE)
                kk = pl.multiple_of(k * TILE, TILE)
                tile = values[t]
                a[pl.ds(rr, TILE), pl.ds(kk, TILE)] = tile
                at[pl.ds(kk, TILE), pl.ds(rr, TILE)] = jnp.transpose(tile)

            return carry

        lax.fori_loop(0, values.shape[0], body, 0)


def product_kernel(parts, *refs):
    lhs, rhs, out = refs[0], refs[1 : 1 + parts], refs[1 + parts]
    total = None
    at = 0
    for ref in rhs:
        depth = ref.shape[0]
        one = jnp.dot(lhs[:, at : at + depth], ref[...], preferred_element_type=F32)
        total = one if total is None else total + one
        at += depth
    out[...] = total.astype(out.dtype)


def product(lhs, rhs, first, rows, block=256):
    depth, width = lhs.shape[1], rhs[0].shape[1]
    skip = first // block
    return call(
        functools.partial(product_kernel, len(rhs)),
        jax.ShapeDtypeStruct((rows, width), BF16),
        [pl.BlockSpec((block, depth), lambda i: (skip + i, 0))]
        + [pl.BlockSpec(r.shape, lambda i: (0, 0)) for r in rhs],
        pl.BlockSpec((block, width), lambda i: (i, 0)),
        grid=(rows // block,),
        flops=2 * rows * depth * width,
        bytes_accessed=2 * (rows * depth + depth * width + rows * width),
    )(lhs, *rhs)


def unit_groups(total):
    power = jnp.mean(total * total, axis=-1, keepdims=True)
    return (total * lax.rsqrt(power + epsilon)).astype(BF16)


def encode_kernel(mix, *refs):
    parts, out = refs[:-1], refs[-1]
    for g in range(out.shape[1] // CH):
        span = slice(g * CH, (g + 1) * CH)
        total = parts[0][:, span].astype(F32)
        for ref in parts[1:]:
            total = total + ref[:, span].astype(F32)
        v = jnp.dot(unit_groups(total), mix[...], preferred_element_type=F32)
        out[:, span] = (0.5 * v * (1.0 + lax.erf(v * (0.5**0.5)))).astype(BF16)


def decode_kernel(parts, mix, x, *refs):
    sums, outs = refs[:parts], refs[parts:]
    for g in range(x.shape[1] // CH):
        span = slice(g * CH, (g + 1) * CH)
        total = sums[0][:, span].astype(F32)
        for ref in sums[1:]:
            total = total + ref[:, span].astype(F32)
        recon = jnp.dot(unit_groups(total), mix[...], preferred_element_type=F32)
        left = x[:, span].astype(F32) - recon
        for i, out in enumerate(outs):
            out[:, span] = left[i * PIECE : (i + 1) * PIECE, :].astype(out.dtype)


def join_kernel(lay, chunks, me, *refs):
    out = refs[-1]
    mine = me[2]
    for n, (first, many) in enumerate(chunks):
        for rel in range(4):
            at = pl.multiple_of((mine ^ rel) * lay.qw + first * CH, CH)
            out[:, pl.ds(at, many * CH)] = refs[n * 4 + rel][...].astype(F32)


CHUNKS = ((0, 3),)


def local(lay, ingest_features, node_map, unit_rows, tile_ids, tile_values, mix_in, mix_out):
    z, c = lax.axis_index("row"), lax.axis_index("col")
    h, l = lay.split_z(z)
    me = jnp.stack(
        [z * lay.C + c, unit_rows[0], h * 2 + c % 2, h, l, c // 2, c % 2]
    ).astype(jnp.int32)

    def exchange(x, dh=0, dl=0, chip=0, core=0):
        pairs = []
        for zz in range(lay.R):
            hh, ll = lay.split_z(zz)
            for cc in range(lay.C):
                to = lay.join_z(hh ^ dh, ll ^ dl) * lay.C + (cc ^ (chip * 2 + core))
                pairs.append((zz * lay.C + cc, to))
        return lax.ppermute(x, ("row", "col"), pairs)

    chunks = tuple((f, min(m, lay.groups - f)) for f, m in CHUNKS)

    outgoing = call(
        functools.partial(pack_kernel, lay),
        jax.ShapeDtypeStruct((lay.U, lay.pay, CH), BF16),
        [SM, VM, VM],
    )(me, node_map.reshape(1, lay.slots), ingest_features)
    got = lax.all_to_all(outgoing, ("row", "col"), split_axis=0, concat_axis=0, tiled=True)

    ids0 = tile_ids.reshape(-1)
    ids1, val1 = exchange(ids0, dh=1), exchange(tile_values, dh=1)
    ids2, val2 = exchange(ids0, core=1), exchange(tile_values, core=1)
    ids3, val3 = exchange(ids1, core=1), exchange(val1, core=1)

    depth = lay.chips * lay.own
    step_rows = depth if depth * lay.chip_cols <= 2048 * 1024 else lay.own
    held = pl.BlockSpec(tile_values.shape, lambda i: (0, 0, 0))
    a, at = call(
        functools.partial(dense_kernel, lay, step_rows),
        [
            jax.ShapeDtypeStruct((depth, lay.chip_cols), BF16),
            jax.ShapeDtypeStruct((lay.chip_cols, depth), BF16),
        ],
        [SM] * 5 + [held] * 4,
        [
            pl.BlockSpec((step_rows, lay.chip_cols), lambda i: (i, 0)),
            pl.BlockSpec((lay.chip_cols, step_rows), lambda i: (0, i)),
        ],
        grid=(depth // step_rows,),
    )(me, ids0, ids1, ids2, ids3, tile_values, val1, val2, val3)

    own = call(
        functools.partial(land_kernel, lay, chunks),
        [jax.ShapeDtypeStruct((lay.own, m * CH), BF16) for _, m in chunks],
        [SM, VM],
    )(me, got)

    share = lay.chip_cols // lay.R2
    pieces = []
    for x in own:
        width = x.shape[1]
        xs = [x] + [exchange(x, chip=s) for s in range(1, lay.chips)]
        back = [
            exchange(product(at, xs, s * share, share), dl=s) for s in range(1, lay.R2)
        ]
        back = [product(at, xs, 0, share)] + back
        hidden = call(
            encode_kernel,
            jax.ShapeDtypeStruct((share, width), BF16),
            [VM] * (1 + lay.R2),
        )(mix_in, *back)
        hs = [hidden] + [exchange(hidden, dl=s) for s in range(1, lay.R2)]
        forward = [
            exchange(product(a, hs, s * lay.own, lay.own), chip=s)
            for s in range(1, lay.chips)
        ]
        forward = [product(a, hs, 0, lay.own)] + forward
        left = call(
            functools.partial(decode_kernel, lay.chips),
            [
                jax.ShapeDtypeStruct((PIECE, width), F32 if i == 0 else BF16)
                for i in range(4)
            ],
            [VM] * (2 + lay.chips),
        )(mix_out, x, *forward)
        pieces += [
            left[0],
            exchange(left[1], core=1),
            exchange(left[2], dh=1),
            exchange(left[3], dh=1, core=1),
        ]
    return call(
        functools.partial(join_kernel, lay, chunks),
        jax.ShapeDtypeStruct((PIECE, QUARTERS * lay.qw), F32),
        [SM] + [VM] * len(pieces),
    )(me, *pieces)


def solution(mesh):
    rows, cols = mesh.shape["row"], mesh.shape["col"]

    def run(ingest_features, node_map, *rest):
        lay = Layout(
            rows, cols, node_map.shape[0] // (rows * cols), ingest_features.shape[1]
        )
        return jax.shard_map(
            functools.partial(local, lay),
            mesh=mesh,
            in_specs=(
                P(("row", "col"), None),
                P(("row", "col")),
                P(("row", "col")),
                P(("row", "col"), None),
                P(("row", "col"), None, None),
                P(),
                P(),
            ),
            out_specs=P(("row", "col"), None),
            check_vma=False,
        )(ingest_features, node_map, *rest)

    return run
```

```python
import functools

import jax
import jax.numpy as jnp
from jax import lax
from jax.experimental import pallas as pl
from jax.experimental.pallas import tpu as pltpu
from jax.sharding import PartitionSpec as P

CH = 128
TILE = 128
PIECE = 128
QUARTERS = 4
VMEM_LIMIT = [16 * 1024 * 1024]

epsilon = 1e-05

BF16 = jnp.bfloat16
F32 = jnp.float32
VM = pl.BlockSpec(memory_space=pltpu.VMEM)
SM = pl.BlockSpec(memory_space=pltpu.SMEM)


def over(x, n):
    assert n & (n - 1) == 0
    return x >> (n.bit_length() - 1)


def rest(x, n):
    assert n & (n - 1) == 0
    return x & (n - 1)


def iota(shape, axis):
    return lax.broadcasted_iota(jnp.int32, shape, axis)


def call(kernel, out_shape, in_specs, behind=(), flops=0):
    count, many = len(in_specs), len(out_shape)

    def body(*refs):
        kernel(*refs[:count], *refs[count + len(behind) : -1])
        refs[-1][...] = jnp.zeros_like(refs[-1])

    run = pl.pallas_call(
        body,
        out_shape=list(out_shape) + [jax.ShapeDtypeStruct((8, CH), F32)],
        in_specs=list(in_specs) + [VM] * len(behind),
        out_specs=[VM] * (many + 1),
        compiler_params=pltpu.CompilerParams(vmem_limit_bytes=VMEM_LIMIT[0]),
        cost_estimate=pl.CostEstimate(flops=flops, bytes_accessed=0, transcendentals=0),
    )

    def apply(*args):
        *outs, token = run(*args, *behind)
        return outs, token

    return apply


def array(rows, columns, dtype=BF16):
    return jax.ShapeDtypeStruct((rows, columns), dtype)


class Layout:
    def __init__(self, rows, cols, slots, width):
        self.R, self.C = rows, cols
        self.R2, self.chips = rows // 2, cols // 2
        self.U = rows * cols
        self.slots = slots
        self.pair = slots // self.U
        self.slab = 4 * self.pair
        self.upl = CH // self.slab
        self.groups = width // CH // QUARTERS
        self.qw = self.groups * CH
        self.blocks = self.R2 * self.chips
        self.own = 4 * PIECE
        self.chip_cols = 2 * rows * TILE
        self.pay = self.groups * self.slab + 8

    def split_z(self, z):
        return rest(z, 2), over(z, 2)

    def join_z(self, h, l):
        return l * 2 + h


def pack_kernel(lay, me, node, feats, out):
    unit, count = me[0], me[1]
    n = lay.slots
    row = node[...]
    slot = iota((1, n), 1)
    live = slot < count
    p = row // PIECE
    h, l = lay.split_z(p // lay.C)
    c = p % lay.C
    block = l * lay.chips + c // 2
    part = h * 2 + c % 2
    p = jnp.where(live, p, -1)
    across = jnp.broadcast_to(p, (n, n))
    down = jnp.transpose(across)
    before = (across == down) & (iota((n, n), 0) < iota((n, n), 1))
    rank = jnp.sum(jnp.where(before, 1, 0), axis=0, keepdims=True)
    target = jnp.where(live, (block * 4 + part) * lay.pair + rank, -1)
    pick = jnp.where(iota((n, n), 0) == target, 1.0, 0.0).astype(BF16)
    sorted_rows = jnp.dot(pick, feats[...], preferred_element_type=F32).astype(BF16)
    place = jnp.where(live, row % PIECE + 1, 0).astype(F32).astype(BF16)
    place = jnp.broadcast_to(place, (16, n))
    lane = iota((lay.blocks * CH, n), 0)
    inner = lane % CH - (unit % lay.upl) * lay.slab
    wanted = (lane // CH) * lay.slab + inner
    wanted = jnp.where((inner >= 0) & (inner < lay.slab), wanted, -2)
    spread = jnp.where(wanted == target, 1.0, 0.0).astype(BF16)
    places = lax.dot_general(
        place, spread, (((1,), (1,)), ((), ())), preferred_element_type=F32
    ).astype(BF16)
    for z in range(lay.R):
        dh, dl = lay.split_z(z)
        for c in range(lay.C):
            b = dl * lay.chips + c // 2
            q = dh * 2 + c % 2
            d = z * lay.C + c
            for g in range(lay.groups):
                lo = q * lay.qw + g * CH
                out[d, g * lay.slab : (g + 1) * lay.slab, :] = sorted_rows[
                    b * lay.slab : (b + 1) * lay.slab, lo : lo + CH
                ]
            out[d, lay.groups * lay.slab : lay.pay, :] = places[0:8, b * CH : (b + 1) * CH]


def land_kernel(lay, first, many, me, got, out):
    mine = me[2]
    lane = iota((1, CH), 1)
    part = (lane % lay.slab) // lay.pair
    base = (part ^ mine) * PIECE - 1
    rows = iota((lay.own, CH), 0)
    picks = []
    for j in range(lay.U // lay.upl):
        total = jnp.zeros((8, CH), F32)
        for i in range(lay.upl):
            total = total + got[j * lay.upl + i, lay.groups * lay.slab : lay.pay, :].astype(F32)
        place = total[0:1, :].astype(jnp.int32)
        spot = jnp.where(place > 0, base + place, -1)
        picks.append(jnp.where(rows == spot, 1.0, 0.0).astype(BF16))
    pick = jnp.concatenate(picks, axis=1)
    for g in range(many):
        lo = (first + g) * lay.slab
        block = got[:, lo : lo + lay.slab, :].reshape(lay.U * lay.slab, CH)
        out[:, g * CH : (g + 1) * CH] = jnp.dot(
            pick, block, preferred_element_type=F32
        ).astype(BF16)


def dense_kernel(lay, me, i0, i1, i2, i3, v0, v1, v2, v3, a0, at0, a1, at1):
    chip, core = me[3], me[4]
    for ref in (a0, at0, a1, at1):
        ref[...] = jnp.zeros_like(ref)
    spare = 2 * lay.chips
    for ids, values, a, at in ((i0, v0, a0, at0), (i1, v1, a1, at1), (i2, v2, a0, at0), (i3, v3, a1, at1)):

        def body(t, carry, ids=ids, values=values, a=a, at=at):
            rt, ct = ids[0, t], ids[1, t]
            c = rest(rt, lay.C)
            r = (over(c, 2) ^ chip) * 2 + (rest(c, 2) ^ core)
            j = rest(over(ct, lay.R), 2) * lay.R + rest(ct, lay.R)
            r = jnp.where(rt < lay.U, r, spare)
            rr = pl.multiple_of(r * TILE, TILE)
            kk = pl.multiple_of(j * TILE, TILE)
            tile = values[t]
            a[pl.ds(rr, TILE), pl.ds(kk, TILE)] = tile
            at[pl.ds(kk, TILE), pl.ds(rr, TILE)] = jnp.transpose(tile)
            return carry

        lax.fori_loop(0, values.shape[0], body, 0, unroll=4)


def seen_kernel(*refs):
    pass


def back_kernel(chips, lo, width, *refs):
    at0, at1, xs, out = refs[0], refs[1], refs[2 : 2 + chips], refs[2 + chips]
    span = slice(lo, lo + width)
    near = jnp.concatenate([x[0 : 2 * PIECE, span] for x in xs], axis=0)
    depth = near.shape[0]
    far = jnp.concatenate([x[2 * PIECE : 4 * PIECE, span] for x in xs], axis=0)
    for lo in range(0, out.shape[0], BLOCK):
        rows = slice(lo, lo + BLOCK)
        total = jnp.dot(at0[rows, 0:depth], near, preferred_element_type=F32)
        total += jnp.dot(at1[rows, 0:depth], far, preferred_element_type=F32)
        out[rows, :] = total.astype(BF16)


def forward_kernel(first, a0, a1, hidden, *outs):
    for i, out in enumerate(outs):
        rows = slice((first + i) * 2 * PIECE, (first + i + 1) * 2 * PIECE)
        for lo, a in ((0, a0), (2 * PIECE, a1)):
            total = jnp.dot(a[rows, :], hidden[...], preferred_element_type=F32)
            out[lo : lo + 2 * PIECE, :] = total.astype(BF16)


def unit_groups(total):
    power = jnp.mean(total * total, axis=-1, keepdims=True)
    return (total * lax.rsqrt(power + epsilon)).astype(BF16)


def encode_kernel(mix, *refs):
    parts, out = refs[:-1], refs[-1]
    for g in range(out.shape[1] // CH):
        span = slice(g * CH, (g + 1) * CH)
        total = parts[0][:, span].astype(F32)
        for ref in parts[1:]:
            total = total + ref[:, span].astype(F32)
        v = jnp.dot(unit_groups(total), mix[...], preferred_element_type=F32)
        out[:, span] = (0.5 * v * (1.0 + lax.erf(v * (0.5**0.5)))).astype(BF16)


def decode_kernel(parts, takes, lo, done, mix, *refs):
    xs, totals = refs[:takes], refs[takes : takes + parts]
    early, outs = refs[takes + parts : -4], refs[-4:]
    for out, ref in zip(outs, early):
        out[:, 0:done] = ref[...]
    x_at = [(x, at) for x in xs for at in range(0, x.shape[1], CH)][lo // CH :]
    for g in range(totals[0].shape[1] // CH):
        span = slice(g * CH, (g + 1) * CH)
        total = totals[0][:, span].astype(F32)
        for ref in totals[1:]:
            total = total + ref[:, span].astype(F32)
        recon = jnp.dot(unit_groups(total), mix[...], preferred_element_type=F32)
        x, at = x_at[g]
        left = x[:, at : at + CH].astype(F32) - recon
        for i, out in enumerate(outs):
            to = slice(done + g * CH, done + (g + 1) * CH)
            out[:, to] = left[i * PIECE : (i + 1) * PIECE, :].astype(out.dtype)


def join_kernel(lay, me, *refs):
    out = refs[-1]
    for rel in range(4):
        at = pl.multiple_of((me[2] ^ rel) * lay.qw, CH)
        out[:, pl.ds(at, lay.qw)] = refs[rel][...].astype(F32)


GATHER = ((0, 1), (1, 2))
SUMS = ((0, 1), (1, 1), (2, 1))
BLOCK = 256
SEEN_FLOPS = 3_000_000_000
FIRST_FLOPS = 5_000_000_000
DECODE_FLOPS = 3_000_000_000


def inside(parts, first, many):
    for n, (f, m) in enumerate(parts):
        if f <= first and first + many <= f + m:
            return n, (first - f) * CH
    raise ValueError("not nested")


def local(lay, ingest_features, node_map, unit_rows, tile_ids, tile_values, mix_in, mix_out):
    z, c = lax.axis_index("row"), lax.axis_index("col")
    me = jnp.stack(
        [z * lay.C + c, unit_rows[0], rest(z, 2) * 2 + rest(c, 2), over(c, 2), rest(c, 2)]
    ).astype(jnp.int32)

    def exchange(x, dh=0, dl=0, chip=0, core=0):
        pairs = []
        for zz in range(lay.R):
            hh, ll = lay.split_z(zz)
            for cc in range(lay.C):
                to = lay.join_z(hh ^ dh, ll ^ dl) * lay.C + (cc ^ (chip * 2 + core))
                pairs.append((zz * lay.C + cc, to))
        return lax.ppermute(x, ("row", "col"), pairs)

    ids0 = tile_ids.T
    ids1, val1 = exchange(ids0, dh=1), exchange(tile_values, dh=1)
    ids2, val2 = exchange(ids0, core=1), exchange(tile_values, core=1)
    ids3 = exchange(ids1, core=1)

    (outgoing,), _ = call(
        functools.partial(pack_kernel, lay),
        [jax.ShapeDtypeStruct((lay.U, lay.pay, CH), BF16)],
        [SM, VM, VM],
    )(me, node_map.reshape(1, lay.slots), ingest_features)
    got = lax.all_to_all(outgoing, ("row", "col"), split_axis=0, concat_axis=0, tiled=True)

    val3 = exchange(val1, core=1)
    ids, values = (ids0, ids1, ids2, ids3), (tile_values, val1, val2, val3)
    _, token = call(seen_kernel, [], [SM] * 3 + [VM], flops=SEEN_FLOPS)(ids1, ids2, ids3, val3)

    def land(first, many, token):
        (x,), token = call(
            functools.partial(land_kernel, lay, first, many),
            [array(lay.own, many * CH)],
            [SM, VM],
            behind=[token],
        )(me, got)
        return [x] + [exchange(x, chip=s) for s in range(1, lay.chips)], token

    xs, token = land(*GATHER[0], token)
    gathered = [xs]
    depth = 2 * lay.chips * PIECE + TILE
    (a0, at0, a1, at1), token = call(
        functools.partial(dense_kernel, lay),
        [array(depth, lay.chip_cols), array(lay.chip_cols, depth)] * 2,
        [SM] * 5 + [VM] * 4,
        behind=[token],
    )(me, *ids, *values)
    for first, many in GATHER[1:]:
        xs, token = land(first, many, token)
        gathered.append(xs)
    own = [xs[0] for xs in gathered]

    def back(n, token):
        first, many = SUMS[n]
        where, lo = inside(GATHER, first, many)
        (mine,), token = call(
            functools.partial(back_kernel, lay.chips, lo, many * CH),
            [array(lay.chip_cols, many * CH)],
            [VM] * (2 + lay.chips),
            behind=[token],
            flops=0 if n else FIRST_FLOPS,
        )(at0, at1, *gathered[where])
        return [mine] + [exchange(mine, dl=s) for s in range(1, lay.R2)], token

    def forward(sums, token):
        shape = sums[0].shape
        (hidden,), token = call(
            encode_kernel, [array(*shape)], [VM] * (1 + lay.R2), behind=[token]
        )(mix_in, *sums)
        sent, token = call(
            functools.partial(forward_kernel, 1),
            [array(lay.own, shape[1])] * (lay.chips - 1),
            [VM] * 3,
            behind=[token],
        )(a0, a1, hidden)
        kept, token = call(
            functools.partial(forward_kernel, 0),
            [array(lay.own, shape[1])],
            [VM] * 3,
            behind=[token],
        )(a0, a1, hidden)
        return kept + [exchange(f, chip=s + 1) for s, f in enumerate(sent)], token

    def decode(n, parts, left, token, flops=0):
        first, many = SUMS[n]
        done = first * CH
        return call(
            functools.partial(decode_kernel, lay.chips, len(own), done, done),
            [array(PIECE, done + many * CH, F32 if i == 0 else BF16) for i in range(4)],
            [VM] * (1 + len(own) + lay.chips + len(left)),
            behind=[token],
            flops=flops,
        )(mix_out, *own, *parts, *left)

    left, parts = [], []
    sums, token = back(0, token)
    for n in range(len(SUMS)):
        if n == 0:
            later, token = back(1, token)
        part, token = forward(sums, token)
        parts.append(part)
        if n > 0:
            left, token = decode(n - 1, parts[n - 1], left, token, DECODE_FLOPS)
        if n + 2 < len(SUMS):
            sums = later
            later, token = back(n + 2, token)
        else:
            sums = later
    left, token = decode(len(SUMS) - 1, parts[-1], left, token)
    pieces = [
        left[0],
        exchange(left[1], core=1),
        exchange(left[2], dh=1),
        exchange(left[3], dh=1, core=1),
    ]
    (out,), _ = call(
        functools.partial(join_kernel, lay),
        [array(PIECE, QUARTERS * lay.qw, F32)],
        [SM] + [VM] * 4,
    )(me, *pieces)
    return out


def solution(mesh):
    rows, cols = mesh.shape["row"], mesh.shape["col"]

    def run(ingest_features, node_map, *rest):
        VMEM_LIMIT[0] = (16 if rows * cols <= 32 else 56) * 1024 * 1024
        lay = Layout(
            rows, cols, node_map.shape[0] // (rows * cols), ingest_features.shape[1]
        )
        return jax.shard_map(
            functools.partial(local, lay),
            mesh=mesh,
            in_specs=(
                P(("row", "col"), None),
                P(("row", "col")),
                P(("row", "col")),
                P(("row", "col"), None),
                P(("row", "col"), None, None),
                P(),
                P(),
            ),
            out_specs=P(("row", "col"), None),
            check_vma=False,
        )(ingest_features, node_map, *rest)

    return run
```

```python
import functools

import jax
import jax.numpy as jnp
from jax import lax
from jax.experimental import pallas as pl
from jax.experimental.pallas import tpu as pltpu
from jax.sharding import PartitionSpec as P

CH = 128
TILE = 128
PIECE = 128
QUARTERS = 4
VMEM_LIMIT = [16 * 1024 * 1024]

epsilon = 1e-05

BF16 = jnp.bfloat16
F32 = jnp.float32
VM = pl.BlockSpec(memory_space=pltpu.VMEM)
SM = pl.BlockSpec(memory_space=pltpu.SMEM)
HB = pl.BlockSpec(memory_space=pltpu.HBM)


def over(x, n):
    assert n & (n - 1) == 0
    return x >> (n.bit_length() - 1)


def rest(x, n):
    assert n & (n - 1) == 0
    return x & (n - 1)


def iota(shape, axis):
    return lax.broadcasted_iota(jnp.int32, shape, axis)


def call(kernel, out_shape, in_specs, behind=(), flops=0, scratch=(), vmem=None):
    count, many = len(in_specs), len(out_shape)
    last = count + len(behind) + many

    def body(*refs):
        kernel(*refs[:count], *refs[count + len(behind) : last], *refs[last + 1 :])
        refs[last][...] = jnp.zeros_like(refs[last])

    run = pl.pallas_call(
        body,
        out_shape=list(out_shape) + [jax.ShapeDtypeStruct((8, CH), F32)],
        in_specs=list(in_specs) + [VM] * len(behind),
        out_specs=[VM] * (many + 1),
        scratch_shapes=list(scratch),
        compiler_params=pltpu.CompilerParams(vmem_limit_bytes=vmem or VMEM_LIMIT[0]),
        cost_estimate=pl.CostEstimate(flops=flops, bytes_accessed=0, transcendentals=0),
    )

    def apply(*args):
        *outs, token = run(*args, *behind)
        return outs, token

    return apply


def array(rows, columns, dtype=BF16):
    return jax.ShapeDtypeStruct((rows, columns), dtype)


class Layout:
    def __init__(self, rows, cols, slots, width):
        self.R, self.C = rows, cols
        self.R2, self.chips = rows // 2, cols // 2
        self.U = rows * cols
        self.slots = slots
        self.pair = slots // self.U
        self.slab = 4 * self.pair
        self.upl = CH // self.slab
        self.groups = width // CH // QUARTERS
        self.qw = self.groups * CH
        self.blocks = self.R2 * self.chips
        self.own = 4 * PIECE
        self.chip_cols = 2 * rows * TILE
        self.pay = self.groups * self.slab + 8

    def split_z(self, z):
        return rest(z, 2), over(z, 2)

    def join_z(self, h, l):
        return l * 2 + h


def pack_kernel(lay, me, node, tiles, feats_far, out, feats, ids, arrived):
    unit, count = me[0], me[1]
    n = lay.slots
    bring = pltpu.make_async_copy(feats_far, feats, arrived)
    bring.start()
    ids[...] = jnp.zeros_like(ids)
    ids[1:3, 0 : tiles.shape[1]] = tiles[...]
    row = node[...]
    slot = iota((1, n), 1)
    live = slot < count
    p = row // PIECE
    h, l = lay.split_z(p // lay.C)
    c = p % lay.C
    block = l * lay.chips + c // 2
    part = h * 2 + c % 2
    p = jnp.where(live, p, -1)
    across = jnp.broadcast_to(p, (n, n))
    down = jnp.transpose(across)
    before = (across == down) & (iota((n, n), 0) < iota((n, n), 1))
    rank = jnp.sum(jnp.where(before, 1, 0), axis=0, keepdims=True)
    target = jnp.where(live, (block * 4 + part) * lay.pair + rank, -1)
    pick = jnp.where(iota((n, n), 0) == target, 1.0, 0.0).astype(BF16)
    place = jnp.where(live, row % PIECE + 1, 0).astype(F32).astype(BF16)
    place = jnp.broadcast_to(place, (16, n))
    lane = iota((lay.blocks * CH, n), 0)
    inner = lane % CH - (unit % lay.upl) * lay.slab
    wanted = (lane // CH) * lay.slab + inner
    wanted = jnp.where((inner >= 0) & (inner < lay.slab), wanted, -2)
    spread = jnp.where(wanted == target, 1.0, 0.0).astype(BF16)
    places = lax.dot_general(
        place, spread, (((1,), (1,)), ((), ())), preferred_element_type=F32
    )[0:8]
    top = iota((8, CH), 0) == 0
    lower = ids[...].astype(F32)
    bring.wait()
    sorted_rows = jnp.dot(pick, feats[...], preferred_element_type=F32).astype(BF16)
    below = [
        jnp.where(top, places[:, b * CH : (b + 1) * CH], lower).astype(BF16)
        for b in range(lay.blocks)
    ]
    for z in range(lay.R):
        dh, dl = lay.split_z(z)
        for c in range(lay.C):
            b = dl * lay.chips + c // 2
            q = dh * 2 + c % 2
            d = z * lay.C + c
            for g in range(lay.groups):
                lo = q * lay.qw + g * CH
                out[d, g * lay.slab : (g + 1) * lay.slab, :] = sorted_rows[
                    b * lay.slab : (b + 1) * lay.slab, lo : lo + CH
                ]
            out[d, lay.groups * lay.slab : lay.pay, :] = below[b]


def land_kernel(lay, first, many, me, got, out, ids=None):
    mine = me[2]
    lane = iota((1, CH), 1)
    part = (lane % lay.slab) // lay.pair
    base = (part ^ mine) * PIECE - 1
    rows = iota((lay.own, CH), 0)
    picks = []
    for j in range(lay.U // lay.upl):
        total = jnp.zeros((8, CH), F32)
        for i in range(lay.upl):
            total = total + got[j * lay.upl + i, lay.groups * lay.slab : lay.pay, :].astype(F32)
        place = total[0:1, :].astype(jnp.int32)
        spot = jnp.where(place > 0, base + place, -1)
        picks.append(jnp.where(rows == spot, 1.0, 0.0).astype(BF16))
    pick = jnp.concatenate(picks, axis=1)
    for g in range(many):
        lo = (first + g) * lay.slab
        block = got[:, lo : lo + lay.slab, :].reshape(lay.U * lay.slab, CH)
        out[:, g * CH : (g + 1) * CH] = jnp.dot(
            pick, block, preferred_element_type=F32
        ).astype(BF16)
    if ids is not None:
        for i in range(4):
            found = got[me[5 + i], lay.groups * lay.slab : lay.pay, :].astype(F32)
            ids[2 * i : 2 * i + 2, :] = found[1:3, :].astype(jnp.int32)


def dense_kernel(lay, turned, me, ids, v0, v1, v2, v3, near, far):
    chip, core = me[3], me[4]
    near[...] = jnp.zeros_like(near)
    far[...] = jnp.zeros_like(far)
    spare = 2 * lay.chips
    for i, (values, to) in enumerate(((v0, near), (v1, far), (v2, near), (v3, far))):

        def body(t, carry, i=i, values=values, to=to):
            rt, ct = ids[2 * i, t], ids[2 * i + 1, t]
            c = rest(rt, lay.C)
            r = (over(c, 2) ^ chip) * 2 + (rest(c, 2) ^ core)
            k = rest(over(ct, lay.R), 2) * lay.R + rest(ct, lay.R)
            r = jnp.where(rt < lay.U, r, spare)
            rr = pl.ds(pl.multiple_of(r * TILE, TILE), TILE)
            kk = pl.ds(pl.multiple_of(k * TILE, TILE), TILE)
            if turned:
                to[kk, rr] = jnp.transpose(values[t])
            else:
                to[rr, kk] = values[t]
            return carry

        lax.fori_loop(0, values.shape[0], body, 0, unroll=4)


def seen_kernel(*refs):
    pass


def back_kernel(chips, lo, width, *refs):
    at0, at1, xs, out = refs[0], refs[1], refs[2 : 2 + chips], refs[2 + chips]
    span = slice(lo, lo + width)
    near = jnp.concatenate([x[0 : 2 * PIECE, span] for x in xs], axis=0)
    depth = near.shape[0]
    far = jnp.concatenate([x[2 * PIECE : 4 * PIECE, span] for x in xs], axis=0)
    for lo in range(0, out.shape[0], BLOCK):
        rows = slice(lo, lo + BLOCK)
        total = jnp.dot(at0[rows, 0:depth], near, preferred_element_type=F32)
        total += jnp.dot(at1[rows, 0:depth], far, preferred_element_type=F32)
        out[rows, :] = total.astype(BF16)


def forward_kernel(first, a0, a1, hidden, *outs):
    for i, out in enumerate(outs):
        rows = slice((first + i) * 2 * PIECE, (first + i + 1) * 2 * PIECE)
        for lo, a in ((0, a0), (2 * PIECE, a1)):
            total = jnp.dot(a[rows, :], hidden[...], preferred_element_type=F32)
            out[lo : lo + 2 * PIECE, :] = total.astype(BF16)


def unit_groups(total):
    power = jnp.mean(total * total, axis=-1, keepdims=True)
    return (total * lax.rsqrt(power + epsilon)).astype(BF16)


def encode_kernel(parts, mix, *refs):
    sums, a0, a1, hidden, outs = refs[:parts], refs[parts], refs[parts + 1], refs[parts + 2], refs[parts + 3 :]
    for g in range(hidden.shape[1] // CH):
        span = slice(g * CH, (g + 1) * CH)
        total = sums[0][:, span].astype(F32)
        for ref in sums[1:]:
            total = total + ref[:, span].astype(F32)
        v = jnp.dot(unit_groups(total), mix[...], preferred_element_type=F32)
        hidden[:, span] = (0.5 * v * (1.0 + lax.erf(v * (0.5**0.5)))).astype(BF16)
    forward_kernel(1, a0, a1, hidden, *outs)


def decode_kernel(parts, takes, lo, done, mix, *refs):
    xs, totals = refs[:takes], refs[takes : takes + parts]
    early, outs = refs[takes + parts : -4], refs[-4:]
    for out, ref in zip(outs, early):
        out[:, 0:done] = ref[...]
    x_at = [(x, at) for x in xs for at in range(0, x.shape[1], CH)][lo // CH :]
    for g in range(totals[0].shape[1] // CH):
        span = slice(g * CH, (g + 1) * CH)
        total = totals[0][:, span].astype(F32)
        for ref in totals[1:]:
            total = total + ref[:, span].astype(F32)
        recon = jnp.dot(unit_groups(total), mix[...], preferred_element_type=F32)
        x, at = x_at[g]
        left = x[:, at : at + CH].astype(F32) - recon
        for i, out in enumerate(outs):
            to = slice(done + g * CH, done + (g + 1) * CH)
            out[:, to] = left[i * PIECE : (i + 1) * PIECE, :].astype(out.dtype)


def join_kernel(lay, me, *refs):
    early, late, out = refs[0:4], refs[4:8], refs[8]
    for rel in range(4):
        at = (me[2] ^ rel) * lay.qw
        for ref in (early[rel], late[rel]):
            width = ref.shape[1]
            out[:, pl.ds(pl.multiple_of(at, CH), width)] = ref[...].astype(F32)
            at += width


GATHER = ((0, 1), (1, 2))
SUMS = ((0, 1), (1, 1), (2, 1))
BLOCK = 256
PACK_VMEM = 58 * 1024 * 1024
SEEN_FLOPS = 3_000_000_000
FIRST_FLOPS = 5_000_000_000
DECODE_FLOPS = 3_000_000_000


def inside(parts, first, many):
    for n, (f, m) in enumerate(parts):
        if f <= first and first + many <= f + m:
            return n, (first - f) * CH
    raise ValueError("not nested")


def local(lay, ingest_features, node_map, unit_rows, tile_ids, tile_values, mix_in, mix_out):
    z, c = lax.axis_index("row"), lax.axis_index("col")
    h, l = lay.split_z(z)
    near = [lay.join_z(h ^ dh, l) * lay.C + (c ^ dc) for dc in (0, 1) for dh in (0, 1)]
    me = jnp.stack(
        [z * lay.C + c, unit_rows[0], h * 2 + rest(c, 2), over(c, 2), rest(c, 2), *near]
    ).astype(jnp.int32)

    def exchange(x, dh=0, dl=0, chip=0, core=0):
        pairs = []
        for zz in range(lay.R):
            hh, ll = lay.split_z(zz)
            for cc in range(lay.C):
                to = lay.join_z(hh ^ dh, ll ^ dl) * lay.C + (cc ^ (chip * 2 + core))
                pairs.append((zz * lay.C + cc, to))
        return lax.ppermute(x, ("row", "col"), pairs)

    val1, val2 = exchange(tile_values, dh=1), exchange(tile_values, core=1)
    val3 = exchange(val1, core=1)
    values = (tile_values, val1, val2, val3)

    (outgoing,), _ = call(
        functools.partial(pack_kernel, lay),
        [jax.ShapeDtypeStruct((lay.U, lay.pay, CH), BF16)],
        [SM, VM, VM, HB],
        scratch=[
            pltpu.VMEM(ingest_features.shape, BF16),
            pltpu.VMEM((8, CH), jnp.int32),
            pltpu.SemaphoreType.DMA(()),
        ],
        vmem=PACK_VMEM,
    )(me, node_map.reshape(1, lay.slots), tile_ids.T, ingest_features)
    got = lax.all_to_all(outgoing, ("row", "col"), split_axis=0, concat_axis=0, tiled=True)

    _, token = call(seen_kernel, [], [VM], flops=SEEN_FLOPS)(val3)

    def land(first, many, token, extra=()):
        (x, *more), token = call(
            functools.partial(land_kernel, lay, first, many),
            [array(lay.own, many * CH), *extra],
            [SM, VM],
            behind=[token],
        )(me, got)
        return [x] + [exchange(x, chip=s) for s in range(1, lay.chips)], more, token

    def dense(turned, token):
        depth = 2 * lay.chips * PIECE + TILE
        shape = (lay.chip_cols, depth) if turned else (depth, lay.chip_cols)
        return call(
            functools.partial(dense_kernel, lay, turned),
            [array(*shape)] * 2,
            [SM] * 2 + [VM] * 4,
            behind=[token],
        )(me, ids, *values)

    xs, (ids,), token = land(*GATHER[0], token, [array(8, CH, jnp.int32)])
    gathered = [xs]
    (at0, at1), token = dense(True, token)
    for first, many in GATHER[1:]:
        xs, _, token = land(first, many, token)
        gathered.append(xs)
    own = [xs[0] for xs in gathered]

    def back(n, token):
        first, many = SUMS[n]
        where, lo = inside(GATHER, first, many)
        (mine,), token = call(
            functools.partial(back_kernel, lay.chips, lo, many * CH),
            [array(lay.chip_cols, many * CH)],
            [VM] * (2 + lay.chips),
            behind=[token],
            flops=0 if n else FIRST_FLOPS,
        )(at0, at1, *gathered[where])
        return [mine] + [exchange(mine, dl=s) for s in range(1, lay.R2)], token

    def forward(sums, token):
        shape = sums[0].shape
        (hidden, *sent), token = call(
            functools.partial(encode_kernel, lay.R2),
            [array(*shape)] + [array(lay.own, shape[1])] * (lay.chips - 1),
            [VM] * (3 + lay.R2),
            behind=[token],
        )(mix_in, *sums, a0, a1)
        kept, _ = call(
            functools.partial(forward_kernel, 0),
            [array(lay.own, shape[1])],
            [VM] * 3,
            behind=[token],
        )(a0, a1, hidden)
        return kept + [exchange(f, chip=s + 1) for s, f in enumerate(sent)], token

    def decode(n, parts, left, token, flops=0):
        first, many = SUMS[n]
        done = left[0].shape[1] if left else 0
        return call(
            functools.partial(decode_kernel, lay.chips, len(own), first * CH, done),
            [array(PIECE, done + many * CH, F32 if i == 0 else BF16) for i in range(4)],
            [VM] * (1 + len(own) + lay.chips + len(left)),
            behind=[token],
            flops=flops,
        )(mix_out, *own, *parts, *left)

    def deliver(left):
        return [
            left[0],
            exchange(left[1], core=1),
            exchange(left[2], dh=1),
            exchange(left[3], dh=1, core=1),
        ]

    left, parts = [], []
    sums, token = back(0, token)
    for n in range(len(SUMS)):
        if n == 0:
            later, token = back(1, token)
            (a0, a1), token = dense(False, token)
        part, token = forward(sums, token)
        parts.append(part)
        if n > 0:
            left, token = decode(n - 1, parts[n - 1], left, token, DECODE_FLOPS)
        sums = later
        if n + 2 < len(SUMS):
            later, token = back(n + 2, token)
    early = deliver(left)
    left, token = decode(len(SUMS) - 1, parts[-1], [], token)
    _, token = call(seen_kernel, [], [VM] * 3, behind=[token], flops=SEEN_FLOPS)(*early[1:])
    pieces = early + deliver(left)
    (out,), _ = call(
        functools.partial(join_kernel, lay),
        [array(PIECE, QUARTERS * lay.qw, F32)],
        [SM] + [VM] * 8,
        behind=[token],
    )(me, *pieces)
    return out


def solution(mesh):
    rows, cols = mesh.shape["row"], mesh.shape["col"]

    def run(ingest_features, node_map, *rest):
        VMEM_LIMIT[0] = (16 if rows * cols <= 32 else 56) * 1024 * 1024
        lay = Layout(
            rows, cols, node_map.shape[0] // (rows * cols), ingest_features.shape[1]
        )
        return jax.shard_map(
            functools.partial(local, lay),
            mesh=mesh,
            in_specs=(
                P(("row", "col"), None),
                P(("row", "col")),
                P(("row", "col")),
                P(("row", "col"), None),
                P(("row", "col"), None, None),
                P(),
                P(),
            ),
            out_specs=P(("row", "col"), None),
            check_vma=False,
        )(ingest_features, node_map, *rest)

    return run
```

```python
import functools

import jax
import jax.numpy as jnp
from jax import lax
from jax.experimental import pallas as pl
from jax.experimental.pallas import tpu as pltpu
from jax.sharding import PartitionSpec as P

CH = 128
TILE = 128
PIECE = 128
QUARTERS = 4
VMEM_LIMIT = [16 * 1024 * 1024]

epsilon = 1e-05

BF16 = jnp.bfloat16
F32 = jnp.float32
VM = pl.BlockSpec(memory_space=pltpu.VMEM)
SM = pl.BlockSpec(memory_space=pltpu.SMEM)
HB = pl.BlockSpec(memory_space=pltpu.HBM)


class Here:
    def __init__(self, lay):
        z, c = lax.axis_index("row"), lax.axis_index("col")
        self.col, self.unit = c, z * lay.C + c
        self.h, self.l = lay.split_z(z)
        self.chip, self.core = over(c, 2), rest(c, 2)
        self.quarter = self.h * 2 + self.core


def over(x, n):
    assert n & (n - 1) == 0
    return x >> (n.bit_length() - 1)


def rest(x, n):
    assert n & (n - 1) == 0
    return x & (n - 1)


def iota(shape, axis):
    return lax.broadcasted_iota(jnp.int32, shape, axis)


def call(kernel, out_shape, in_specs, behind=(), flops=0, scratch=(), vmem=None, out_specs=None, aliases=None):
    count, many = len(in_specs), len(out_shape)
    last = count + len(behind) + many

    def body(*refs):
        kernel(*refs[:count], *refs[count + len(behind) : last], *refs[last + 1 :])
        refs[last][...] = jnp.zeros_like(refs[last])

    run = pl.pallas_call(
        body,
        out_shape=list(out_shape) + [jax.ShapeDtypeStruct((8, CH), F32)],
        in_specs=list(in_specs) + [VM] * len(behind),
        out_specs=list(out_specs or [VM] * many) + [VM],
        input_output_aliases=aliases or {},
        scratch_shapes=list(scratch),
        compiler_params=pltpu.CompilerParams(vmem_limit_bytes=vmem or VMEM_LIMIT[0]),
        cost_estimate=pl.CostEstimate(flops=flops, bytes_accessed=0, transcendentals=0),
    )

    def apply(*args):
        *outs, token = run(*args, *behind)
        return outs, token

    return apply


def array(rows, columns, dtype=BF16):
    return jax.ShapeDtypeStruct((rows, columns), dtype)


class Layout:
    def __init__(self, rows, cols, slots, width):
        self.R, self.C = rows, cols
        self.R2, self.chips = rows // 2, cols // 2
        self.U = rows * cols
        self.slots = slots
        self.pair = slots // self.U
        self.slab = 4 * self.pair
        self.upl = CH // self.slab
        self.groups = width // CH // QUARTERS
        self.qw = self.groups * CH
        self.blocks = self.R2 * self.chips
        self.own = 4 * PIECE
        self.chip_cols = 2 * rows * TILE
        self.pay = self.groups * self.slab + 8

    def split_z(self, z):
        return rest(z, 2), over(z, 2)

    def join_z(self, h, l):
        return l * 2 + h


def pack_kernel(lay, held, node, tiles, feats_far, out_far, out, feats, ids, arrived, gone):
    unit, count = Here(lay).unit, held[0]
    n = lay.slots
    bring = pltpu.make_async_copy(feats_far, feats, arrived)
    bring.start()
    ids[...] = jnp.zeros_like(ids)
    ids[1:3, 0 : tiles.shape[1]] = tiles[...]
    row = node[...]
    slot = iota((1, n), 1)
    live = slot < count
    p = over(row, PIECE)
    h, l = lay.split_z(over(p, lay.C))
    c = rest(p, lay.C)
    block = l * lay.chips + over(c, 2)
    part = h * 2 + rest(c, 2)
    p = jnp.where(live, p, -1)
    across = jnp.broadcast_to(p, (n, n))
    down = jnp.transpose(across)
    before = (across == down) & (iota((n, n), 0) < iota((n, n), 1))
    rank = jnp.sum(jnp.where(before, 1, 0), axis=0, keepdims=True)
    target = jnp.where(live, (block * 4 + part) * lay.pair + rank, -1)
    pick = jnp.where(iota((n, n), 0) == target, 1.0, 0.0).astype(BF16)
    place = jnp.where(live, rest(row, PIECE) + 1, 0).astype(F32).astype(BF16)
    place = jnp.broadcast_to(place, (16, n))
    places = lax.dot_general(
        place, pick, (((1,), (1,)), ((), ())), preferred_element_type=F32
    )
    block = over(iota((lay.blocks, n), 1), lay.slab) == iota((lay.blocks, n), 0)
    place = jnp.where(block, places[0:1, :], 0.0).astype(BF16)
    fro, to = iota((n, CH), 0), iota((n, CH), 1)
    move = (rest(fro, lay.slab) == rest(to, lay.slab)) & (
        over(to, lay.slab) == rest(unit, lay.upl)
    )
    move = jnp.where(move, 1.0, 0.0).astype(BF16)
    places = jnp.dot(place, move, preferred_element_type=F32)
    top = iota((8, CH), 0) == 0
    lower = ids[...].astype(F32)
    bring.wait()
    below = [
        jnp.where(top, places[b : b + 1, :], lower).astype(BF16)
        for b in range(lay.blocks)
    ]
    for q in range(QUARTERS):
        ordered = jnp.dot(
            pick, feats[:, q * lay.qw : (q + 1) * lay.qw], preferred_element_type=F32
        ).astype(BF16)
        for l in range(lay.R2):
            for chip in range(lay.chips):
                b = l * lay.chips + chip
                d = lay.join_z(q // 2, l) * lay.C + chip * 2 + q % 2
                for g in range(lay.groups):
                    out[d, g * lay.slab : (g + 1) * lay.slab, :] = ordered[
                        b * lay.slab : (b + 1) * lay.slab, g * CH : (g + 1) * CH
                    ]
                out[d, lay.groups * lay.slab : lay.pay, :] = below[b]
                pltpu.make_async_copy(out.at[d], out_far.at[d], gone.at[d]).start()
    for d in range(lay.U):
        pltpu.make_async_copy(out.at[d], out_far.at[d], gone.at[d]).wait()


def land_kernel(lay, first, many, got, out, ids=None):
    here = Here(lay)
    lane = iota((1, CH), 1)
    part = (lane % lay.slab) // lay.pair
    base = (part ^ here.quarter) * PIECE - 1
    rows = iota((lay.own, CH), 0)
    picks = []
    for j in range(lay.U // lay.upl):
        total = jnp.zeros((8, CH), F32)
        for i in range(lay.upl):
            total = total + got[j * lay.upl + i, lay.groups * lay.slab : lay.pay, :].astype(F32)
        place = total[0:1, :].astype(jnp.int32)
        spot = jnp.where(place > 0, base + place, -1)
        picks.append(jnp.where(rows == spot, 1.0, 0.0).astype(BF16))
    pick = jnp.concatenate(picks, axis=1)
    for g in range(many):
        lo = (first + g) * lay.slab
        block = got[:, lo : lo + lay.slab, :].reshape(lay.U * lay.slab, CH)
        out[:, g * CH : (g + 1) * CH] = jnp.dot(
            pick, block, preferred_element_type=F32
        ).astype(BF16)
    if ids is not None:
        for i in range(4):
            z = lay.join_z(here.h ^ (i % 2), here.l)
            found = got[z * lay.C + (here.col ^ (i // 2)), lay.groups * lay.slab : lay.pay, :].astype(F32)
            ids[2 * i : 2 * i + 2, :] = found[1:3, :].astype(jnp.int32)


def dense_kernel(lay, turned, ids, v0, v1, v2, v3, near, far):
    here = Here(lay)
    near[...] = jnp.zeros_like(near)
    far[...] = jnp.zeros_like(far)
    spare = 2 * lay.chips
    for i, (values, to) in enumerate(((v0, near), (v1, far), (v2, near), (v3, far))):

        def body(t, carry, i=i, values=values, to=to):
            rt, ct = ids[2 * i, t], ids[2 * i + 1, t]
            c = rest(rt, lay.C)
            r = (over(c, 2) ^ here.chip) * 2 + (rest(c, 2) ^ here.core)
            k = rest(over(ct, lay.R), 2) * lay.R + rest(ct, lay.R)
            r = jnp.where(rt < lay.U, r, spare)
            rr = pl.ds(pl.multiple_of(r * TILE, TILE), TILE)
            kk = pl.ds(pl.multiple_of(k * TILE, TILE), TILE)
            if turned:
                to[kk, rr] = jnp.transpose(values[t])
            else:
                to[rr, kk] = values[t]
            return carry

        lax.fori_loop(0, values.shape[0], body, 0, unroll=4)


def seen_kernel(*refs):
    pass


def back_kernel(chips, lo, width, *refs):
    at0, at1, xs, out = refs[0], refs[1], refs[2 : 2 + chips], refs[2 + chips]
    span = slice(lo, lo + width)
    near = jnp.concatenate([x[0 : 2 * PIECE, span] for x in xs], axis=0)
    depth = near.shape[0]
    far = jnp.concatenate([x[2 * PIECE : 4 * PIECE, span] for x in xs], axis=0)
    for lo in range(0, out.shape[0], BLOCK):
        rows = slice(lo, lo + BLOCK)
        total = jnp.dot(at0[rows, 0:depth], near, preferred_element_type=F32)
        total += jnp.dot(at1[rows, 0:depth], far, preferred_element_type=F32)
        out[rows, :] = total.astype(BF16)


def forward_kernel(first, a0, a1, hidden, *outs):
    for i, out in enumerate(outs):
        rows = slice((first + i) * 2 * PIECE, (first + i + 1) * 2 * PIECE)
        for lo, a in ((0, a0), (2 * PIECE, a1)):
            total = jnp.dot(a[rows, :], hidden[...], preferred_element_type=F32)
            out[lo : lo + 2 * PIECE, :] = total.astype(BF16)


def unit_groups(total):
    power = jnp.mean(total * total, axis=-1, keepdims=True)
    return (total * lax.rsqrt(power + epsilon)).astype(BF16)


def encode_kernel(parts, mix, *refs):
    sums, a0, a1, hidden, outs = refs[:parts], refs[parts], refs[parts + 1], refs[parts + 2], refs[parts + 3 :]
    for g in range(hidden.shape[1] // CH):
        span = slice(g * CH, (g + 1) * CH)
        total = sums[0][:, span].astype(F32)
        for ref in sums[1:]:
            total = total + ref[:, span].astype(F32)
        v = jnp.dot(unit_groups(total), mix[...], preferred_element_type=F32)
        hidden[:, span] = (0.5 * v * (1.0 + lax.erf(v * (0.5**0.5)))).astype(BF16)
    forward_kernel(1, a0, a1, hidden, *outs)


def decode_kernel(parts, takes, lo, done, mix, *refs):
    xs, totals = refs[:takes], refs[takes : takes + parts]
    early, outs = refs[takes + parts : -4], refs[-4:]
    for out, ref in zip(outs, early):
        out[:, 0:done] = ref[...]
    x_at = [(x, at) for x in xs for at in range(0, x.shape[1], CH)][lo // CH :]
    for g in range(totals[0].shape[1] // CH):
        span = slice(g * CH, (g + 1) * CH)
        total = totals[0][:, span].astype(F32)
        for ref in totals[1:]:
            total = total + ref[:, span].astype(F32)
        recon = jnp.dot(unit_groups(total), mix[...], preferred_element_type=F32)
        x, at = x_at[g]
        left = x[:, at : at + CH].astype(F32) - recon
        for i, out in enumerate(outs):
            to = slice(done + g * CH, done + (g + 1) * CH)
            out[:, to] = left[i * PIECE : (i + 1) * PIECE, :].astype(out.dtype)


def join_kernel(lay, done, kept, *refs):
    pieces = refs[:4]
    far, wide, gone = refs[-3:]
    mine, width = Here(lay).quarter, pieces[0].shape[1]
    copies = []
    for rel, ref in enumerate(pieces):
        wide[rel] = ref[...].astype(F32)
        at = pl.multiple_of((mine ^ rel) * lay.qw + done, CH)
        copies.append(
            pltpu.make_async_copy(wide.at[rel], far.at[:, pl.ds(at, width)], gone.at[rel])
        )
        copies[-1].start()
    for copy in copies:
        copy.wait()


def first_join_kernel(lay, done, *refs):
    join_kernel(lay, done, None, *refs)


GATHER = ((0, 1), (1, 2))
SUMS = ((0, 1), (1, 1), (2, 1))
BLOCK = 256
PACK_VMEM = 58 * 1024 * 1024
SEEN_FLOPS = 3_000_000_000
FIRST_FLOPS = 5_000_000_000
DECODE_FLOPS = 3_000_000_000


def inside(parts, first, many):
    for n, (f, m) in enumerate(parts):
        if f <= first and first + many <= f + m:
            return n, (first - f) * CH
    raise ValueError("not nested")


def local(lay, ingest_features, node_map, unit_rows, tile_ids, tile_values, mix_in, mix_out):
    def exchange(x, dh=0, dl=0, chip=0, core=0):
        pairs = []
        for zz in range(lay.R):
            hh, ll = lay.split_z(zz)
            for cc in range(lay.C):
                to = lay.join_z(hh ^ dh, ll ^ dl) * lay.C + (cc ^ (chip * 2 + core))
                pairs.append((zz * lay.C + cc, to))
        return lax.ppermute(x, ("row", "col"), pairs)

    val1, val2 = exchange(tile_values, dh=1), exchange(tile_values, core=1)
    val3 = exchange(val1, core=1)
    values = (tile_values, val1, val2, val3)

    (outgoing,), _ = call(
        functools.partial(pack_kernel, lay),
        [jax.ShapeDtypeStruct((lay.U, lay.pay, CH), BF16)],
        [SM, VM, VM, HB],
        out_specs=[HB],
        scratch=[
            pltpu.VMEM((lay.U, lay.pay, CH), BF16),
            pltpu.VMEM(ingest_features.shape, BF16),
            pltpu.VMEM((8, CH), jnp.int32),
            pltpu.SemaphoreType.DMA(()),
            pltpu.SemaphoreType.DMA((lay.U,)),
        ],
        vmem=PACK_VMEM,
    )(unit_rows, node_map.reshape(1, lay.slots), tile_ids.T, ingest_features)
    got = lax.all_to_all(outgoing, ("row", "col"), split_axis=0, concat_axis=0, tiled=True)

    _, token = call(seen_kernel, [], [VM], flops=SEEN_FLOPS)(val3)

    def land(first, many, token, extra=()):
        (x, *more), token = call(
            functools.partial(land_kernel, lay, first, many),
            [array(lay.own, many * CH), *extra],
            [VM],
            behind=[token],
        )(got)
        return [x] + [exchange(x, chip=s) for s in range(1, lay.chips)], more, token

    def dense(turned, token):
        depth = 2 * lay.chips * PIECE + TILE
        shape = (lay.chip_cols, depth) if turned else (depth, lay.chip_cols)
        return call(
            functools.partial(dense_kernel, lay, turned),
            [array(*shape)] * 2,
            [SM] + [VM] * 4,
            behind=[token],
        )(ids, *values)

    xs, (ids,), token = land(*GATHER[0], token, [array(8, CH, jnp.int32)])
    gathered = [xs]
    (at0, at1), token = dense(True, token)
    for first, many in GATHER[1:]:
        xs, _, token = land(first, many, token)
        gathered.append(xs)
    own = [xs[0] for xs in gathered]

    def back(n, token, wait=()):
        first, many = SUMS[n]
        where, lo = inside(GATHER, first, many)
        (mine,), token = call(
            functools.partial(back_kernel, lay.chips, lo, many * CH),
            [array(lay.chip_cols, many * CH)],
            [VM] * (2 + lay.chips),
            behind=[token, *wait],
            flops=0 if n else FIRST_FLOPS,
        )(at0, at1, *gathered[where])
        return [mine] + [exchange(mine, dl=s) for s in range(1, lay.R2)], token

    def forward(sums, token):
        shape = sums[0].shape
        (hidden, *sent), token = call(
            functools.partial(encode_kernel, lay.R2),
            [array(*shape)] + [array(lay.own, shape[1])] * (lay.chips - 1),
            [VM] * (3 + lay.R2),
            behind=[token],
        )(mix_in, *sums, a0, a1)
        kept, _ = call(
            functools.partial(forward_kernel, 0),
            [array(lay.own, shape[1])],
            [VM] * 3,
            behind=[token],
        )(a0, a1, hidden)
        return kept + [exchange(f, chip=s + 1) for s, f in enumerate(sent)], token

    def decode(n, parts, left, token, flops=0):
        first, many = SUMS[n]
        done = left[0].shape[1] if left else 0
        return call(
            functools.partial(decode_kernel, lay.chips, len(own), first * CH, done),
            [array(PIECE, done + many * CH, F32 if i == 0 else BF16) for i in range(4)],
            [VM] * (1 + len(own) + lay.chips + len(left)),
            behind=[token],
            flops=flops,
        )(mix_out, *own, *parts, *left)

    def deliver(left):
        return [
            left[0],
            exchange(left[1], core=1),
            exchange(left[2], dh=1),
            exchange(left[3], dh=1, core=1),
        ]

    left, parts = [], []
    ready, token = back(0, token)
    coming, token = back(1, token)
    (a0, a1), token = dense(False, token)
    for n in range(len(SUMS)):
        following = None
        if n + 2 < len(SUMS):
            following, token = back(n + 2, token, ready[1:])
        part, token = forward(ready, token)
        parts.append(part)
        if n > 0:
            left, token = decode(n - 1, parts[n - 1], left, token, DECODE_FLOPS)
        ready, coming = coming, following
    early = deliver(left)
    left, token = decode(len(SUMS) - 1, parts[-1], [], token)
    late = deliver(left)
    out = None
    for done, pieces in ((0, early), (early[0].shape[1], late)):
        width = pieces[0].shape[1]
        (out,), token = call(
            functools.partial(join_kernel if done else first_join_kernel, lay, done),
            [array(PIECE, QUARTERS * lay.qw, F32)],
            [HB] * (1 if done else 0) + [VM] * 4,
            behind=[token],
            flops=0 if done else SEEN_FLOPS,
            out_specs=[HB],
            scratch=[pltpu.VMEM((4, PIECE, width), F32), pltpu.SemaphoreType.DMA((4,))],
            aliases={0: 0} if done else None,
        )(*([out] if done else []), *pieces)
    return out


def solution(mesh):
    rows, cols = mesh.shape["row"], mesh.shape["col"]

    def run(ingest_features, node_map, *rest):
        VMEM_LIMIT[0] = (16 if rows * cols <= 32 else 56) * 1024 * 1024
        lay = Layout(
            rows, cols, node_map.shape[0] // (rows * cols), ingest_features.shape[1]
        )
        return jax.shard_map(
            functools.partial(local, lay),
            mesh=mesh,
            in_specs=(
                P(("row", "col"), None),
                P(("row", "col")),
                P(("row", "col")),
                P(("row", "col"), None),
                P(("row", "col"), None, None),
                P(),
                P(),
            ),
            out_specs=P(("row", "col"), None),
            check_vma=False,
        )(ingest_features, node_map, *rest)

    return run
```

```python
import functools

import jax
import jax.numpy as jnp
from jax import lax
from jax.experimental import pallas as pl
from jax.experimental.pallas import tpu as pltpu
from jax.sharding import PartitionSpec as P

CH = 128
TILE = 128
PIECE = 128
QUARTERS = 4
VMEM_LIMIT = [16 * 1024 * 1024]

epsilon = 1e-05

BF16 = jnp.bfloat16
F32 = jnp.float32
VM = pl.BlockSpec(memory_space=pltpu.VMEM)
SM = pl.BlockSpec(memory_space=pltpu.SMEM)
HB = pl.BlockSpec(memory_space=pltpu.HBM)


class Here:
    def __init__(self, lay):
        z, c = lax.axis_index("row"), lax.axis_index("col")
        self.col, self.unit = c, z * lay.C + c
        self.h, self.l = lay.split_z(z)
        self.chip, self.core = over(c, 2), rest(c, 2)
        self.quarter = self.h * 2 + self.core


def over(x, n):
    assert n & (n - 1) == 0
    return x >> (n.bit_length() - 1)


def rest(x, n):
    assert n & (n - 1) == 0
    return x & (n - 1)


def iota(shape, axis):
    return lax.broadcasted_iota(jnp.int32, shape, axis)


def call(kernel, out_shape, in_specs, behind=(), flops=0, scratch=(), vmem=None, out_specs=None, aliases=None):
    count, many = len(in_specs), len(out_shape)
    last = count + len(behind) + many

    def body(*refs):
        kernel(*refs[:count], *refs[count + len(behind) : last], *refs[last + 1 :])
        refs[last][...] = jnp.zeros_like(refs[last])

    run = pl.pallas_call(
        body,
        out_shape=list(out_shape) + [jax.ShapeDtypeStruct((8, CH), F32)],
        in_specs=list(in_specs) + [VM] * len(behind),
        out_specs=list(out_specs or [VM] * many) + [VM],
        input_output_aliases=aliases or {},
        scratch_shapes=list(scratch),
        compiler_params=pltpu.CompilerParams(vmem_limit_bytes=vmem or VMEM_LIMIT[0]),
        cost_estimate=pl.CostEstimate(flops=flops, bytes_accessed=0, transcendentals=0),
    )

    def apply(*args):
        *outs, token = run(*args, *behind)
        return outs, token

    return apply


def array(rows, columns, dtype=BF16):
    return jax.ShapeDtypeStruct((rows, columns), dtype)


class Layout:
    def __init__(self, rows, cols, slots, width):
        self.R, self.C = rows, cols
        self.R2, self.chips = rows // 2, cols // 2
        self.U = rows * cols
        self.slots = slots
        self.pair = slots // self.U
        self.slab = 4 * self.pair
        self.upl = CH // self.slab
        self.groups = width // CH // QUARTERS
        self.qw = self.groups * CH
        self.blocks = self.R2 * self.chips
        self.own = 4 * PIECE
        self.chip_cols = 2 * rows * TILE
        self.pay = self.groups * self.slab + 8

    def split_z(self, z):
        return rest(z, 2), over(z, 2)

    def join_z(self, h, l):
        return l * 2 + h


def pack_kernel(lay, held_far, node_far, tiles_far, feats_far, out_far, out, feats, ids, held, node, tiles, arrived, gone):
    unit = Here(lay).unit
    n = lay.slots
    pairs = ((held_far, held), (node_far, node), (tiles_far, tiles), (feats_far, feats))
    first = [pltpu.make_async_copy(a, b, arrived.at[i]) for i, (a, b) in enumerate(pairs)]
    for copy in first:
        copy.start()
    bring = first.pop()
    for copy in first:
        copy.wait()
    count = held[0]
    ids[...] = jnp.zeros_like(ids)
    ids[1:3, 0 : tiles.shape[1]] = tiles[...]
    row = node[...]
    slot = iota((1, n), 1)
    live = slot < count
    p = over(row, PIECE)
    h, l = lay.split_z(over(p, lay.C))
    c = rest(p, lay.C)
    block = l * lay.chips + over(c, 2)
    part = h * 2 + rest(c, 2)
    p = jnp.where(live, p, -1)
    across = jnp.broadcast_to(p, (n, n))
    down = jnp.transpose(across)
    before = (across == down) & (iota((n, n), 0) < iota((n, n), 1))
    rank = jnp.sum(jnp.where(before, 1, 0), axis=0, keepdims=True)
    target = jnp.where(live, (block * 4 + part) * lay.pair + rank, -1)
    pick = jnp.where(iota((n, n), 0) == target, 1.0, 0.0).astype(BF16)
    place = jnp.where(live, rest(row, PIECE) + 1, 0).astype(F32).astype(BF16)
    place = jnp.broadcast_to(place, (16, n))
    places = lax.dot_general(
        place, pick, (((1,), (1,)), ((), ())), preferred_element_type=F32
    )
    block = over(iota((lay.blocks, n), 1), lay.slab) == iota((lay.blocks, n), 0)
    place = jnp.where(block, places[0:1, :], 0.0).astype(BF16)
    fro, to = iota((n, CH), 0), iota((n, CH), 1)
    move = (rest(fro, lay.slab) == rest(to, lay.slab)) & (
        over(to, lay.slab) == rest(unit, lay.upl)
    )
    move = jnp.where(move, 1.0, 0.0).astype(BF16)
    places = jnp.dot(place, move, preferred_element_type=F32)
    top = iota((8, CH), 0) == 0
    lower = ids[...].astype(F32)
    bring.wait()
    below = [
        jnp.where(top, places[b : b + 1, :], lower).astype(BF16)
        for b in range(lay.blocks)
    ]
    for q in range(QUARTERS):
        ordered = jnp.dot(
            pick, feats[:, q * lay.qw : (q + 1) * lay.qw], preferred_element_type=F32
        ).astype(BF16)
        for l in range(lay.R2):
            for chip in range(lay.chips):
                b = l * lay.chips + chip
                d = lay.join_z(q // 2, l) * lay.C + chip * 2 + q % 2
                for g in range(lay.groups):
                    out[d, g * lay.slab : (g + 1) * lay.slab, :] = ordered[
                        b * lay.slab : (b + 1) * lay.slab, g * CH : (g + 1) * CH
                    ]
                out[d, lay.groups * lay.slab : lay.pay, :] = below[b]
                pltpu.make_async_copy(out.at[d], out_far.at[d], gone.at[d]).start()
    for d in range(lay.U):
        pltpu.make_async_copy(out.at[d], out_far.at[d], gone.at[d]).wait()


def land_kernel(lay, first, many, got, out, ids=None):
    here = Here(lay)
    lane = iota((1, CH), 1)
    part = (lane % lay.slab) // lay.pair
    base = (part ^ here.quarter) * PIECE - 1
    rows = iota((lay.own, CH), 0)
    picks = []
    for j in range(lay.U // lay.upl):
        total = jnp.zeros((8, CH), F32)
        for i in range(lay.upl):
            total = total + got[j * lay.upl + i, lay.groups * lay.slab : lay.pay, :].astype(F32)
        place = total[0:1, :].astype(jnp.int32)
        spot = jnp.where(place > 0, base + place, -1)
        picks.append(jnp.where(rows == spot, 1.0, 0.0).astype(BF16))
    pick = jnp.concatenate(picks, axis=1)
    for g in range(many):
        lo = (first + g) * lay.slab
        block = got[:, lo : lo + lay.slab, :].reshape(lay.U * lay.slab, CH)
        out[:, g * CH : (g + 1) * CH] = jnp.dot(
            pick, block, preferred_element_type=F32
        ).astype(BF16)
    if ids is not None:
        for i in range(4):
            z = lay.join_z(here.h ^ (i % 2), here.l)
            found = got[z * lay.C + (here.col ^ (i // 2)), lay.groups * lay.slab : lay.pay, :].astype(F32)
            ids[2 * i : 2 * i + 2, :] = found[1:3, :].astype(jnp.int32)


def dense_kernel(lay, turned, ids, far0, far2, v1, w1, v3, w3, near, far, v0, v2, arrived):
    here = Here(lay)
    fetch = [
        pltpu.make_async_copy(a, b, arrived.at[i]) for i, (a, b) in enumerate(((far0, v0), (far2, v2)))
    ]
    for copy in fetch:
        copy.start()
    near[...] = jnp.zeros_like(near)
    far[...] = jnp.zeros_like(far)
    spare = 2 * lay.chips
    cut = v1.shape[0]
    sets = ((1, 0, v1, far), (3, 0, v3, far), (0, 0, v0, near), (2, 0, v2, near), (1, cut, w1, far), (3, cut, w3, far))
    for i, skip, values, to in sets:
        if i % 2 == 0:
            fetch[i // 2].wait()

        def body(t, carry, i=i, skip=skip, values=values, to=to):
            rt, ct = ids[2 * i, skip + t], ids[2 * i + 1, skip + t]
            c = rest(rt, lay.C)
            r = (over(c, 2) ^ here.chip) * 2 + (rest(c, 2) ^ here.core)
            k = rest(over(ct, lay.R), 2) * lay.R + rest(ct, lay.R)
            r = jnp.where(rt < lay.U, r, spare)
            rr = pl.ds(pl.multiple_of(r * TILE, TILE), TILE)
            kk = pl.ds(pl.multiple_of(k * TILE, TILE), TILE)
            if turned:
                to[kk, rr] = jnp.transpose(values[t])
            else:
                to[rr, kk] = values[t]
            return carry

        lax.fori_loop(0, values.shape[0], body, 0, unroll=min(4, values.shape[0]))


def seen_kernel(*refs):
    pass


def back_kernel(chips, lo, width, *refs):
    at0, at1, xs, out = refs[0], refs[1], refs[2 : 2 + chips], refs[2 + chips]
    span = slice(lo, lo + width)
    near = jnp.concatenate([x[0 : 2 * PIECE, span] for x in xs], axis=0)
    depth = near.shape[0]
    far = jnp.concatenate([x[2 * PIECE : 4 * PIECE, span] for x in xs], axis=0)
    for lo in range(0, out.shape[0], BLOCK):
        rows = slice(lo, lo + BLOCK)
        total = jnp.dot(at0[rows, 0:depth], near, preferred_element_type=F32)
        total += jnp.dot(at1[rows, 0:depth], far, preferred_element_type=F32)
        out[rows, :] = total.astype(BF16)


def forward_kernel(first, a0, a1, hidden, *outs):
    for i, out in enumerate(outs):
        rows = slice((first + i) * 2 * PIECE, (first + i + 1) * 2 * PIECE)
        for lo, a in ((0, a0), (2 * PIECE, a1)):
            total = jnp.dot(a[rows, :], hidden[...], preferred_element_type=F32)
            out[lo : lo + 2 * PIECE, :] = total.astype(BF16)


def unit_groups(total):
    power = jnp.mean(total * total, axis=-1, keepdims=True)
    return (total * lax.rsqrt(power + epsilon)).astype(BF16)


def encode_kernel(parts, mix, *refs):
    sums, a0, a1, hidden, outs = refs[:parts], refs[parts], refs[parts + 1], refs[parts + 2], refs[parts + 3 :]
    for g in range(hidden.shape[1] // CH):
        span = slice(g * CH, (g + 1) * CH)
        total = sums[0][:, span].astype(F32)
        for ref in sums[1:]:
            total = total + ref[:, span].astype(F32)
        v = jnp.dot(unit_groups(total), mix[...], preferred_element_type=F32)
        hidden[:, span] = (0.5 * v * (1.0 + lax.erf(v * (0.5**0.5)))).astype(BF16)
    forward_kernel(1, a0, a1, hidden, *outs)


def decode_kernel(parts, takes, lo, done, mix, *refs):
    xs, totals = refs[:takes], refs[takes : takes + parts]
    early, outs = refs[takes + parts : -4], refs[-4:]
    for out, ref in zip(outs, early):
        out[:, 0:done] = ref[...]
    x_at = [(x, at) for x in xs for at in range(0, x.shape[1], CH)][lo // CH :]
    for g in range(totals[0].shape[1] // CH):
        span = slice(g * CH, (g + 1) * CH)
        total = totals[0][:, span].astype(F32)
        for ref in totals[1:]:
            total = total + ref[:, span].astype(F32)
        recon = jnp.dot(unit_groups(total), mix[...], preferred_element_type=F32)
        x, at = x_at[g]
        left = x[:, at : at + CH].astype(F32) - recon
        for i, out in enumerate(outs):
            to = slice(done + g * CH, done + (g + 1) * CH)
            out[:, to] = left[i * PIECE : (i + 1) * PIECE, :].astype(out.dtype)


def join_kernel(lay, done, kept, *refs):
    pieces = refs[:4]
    far, wide, gone = refs[-3:]
    mine, width = Here(lay).quarter, pieces[0].shape[1]
    copies = []
    for rel, ref in enumerate(pieces):
        wide[rel] = ref[...].astype(F32)
        at = pl.multiple_of((mine ^ rel) * lay.qw + done, CH)
        copies.append(
            pltpu.make_async_copy(wide.at[rel], far.at[:, pl.ds(at, width)], gone.at[rel])
        )
        copies[-1].start()
    for copy in copies:
        copy.wait()


def first_join_kernel(lay, done, *refs):
    join_kernel(lay, done, None, *refs)


GATHER = ((0, 1), (1, 2))
SUMS = ((0, 1), (1, 1), (2, 1))
BLOCK = 256
AHEAD = 5
PACK_VMEM = 58 * 1024 * 1024
SEEN_FLOPS = 7_500_000_000
FIRST_FLOPS = 5_000_000_000
DECODE_FLOPS = 3_000_000_000


def inside(parts, first, many):
    for n, (f, m) in enumerate(parts):
        if f <= first and first + many <= f + m:
            return n, (first - f) * CH
    raise ValueError("not nested")


def local(lay, ingest_features, node_map, unit_rows, tile_ids, tile_values, mix_in, mix_out):
    def exchange(x, dh=0, dl=0, chip=0, core=0):
        pairs = []
        for zz in range(lay.R):
            hh, ll = lay.split_z(zz)
            for cc in range(lay.C):
                to = lay.join_z(hh ^ dh, ll ^ dl) * lay.C + (cc ^ (chip * 2 + core))
                pairs.append((zz * lay.C + cc, to))
        return lax.ppermute(x, ("row", "col"), pairs)

    cut = tile_values.shape[0] * AHEAD // 8
    val1 = [exchange(x, dh=1) for x in (tile_values[:cut], tile_values[cut:])]
    val2 = exchange(tile_values, core=1)
    val3 = [exchange(x, core=1) for x in val1]
    values = (tile_values, val2, *val1, *val3)

    (outgoing,), _ = call(
        functools.partial(pack_kernel, lay),
        [jax.ShapeDtypeStruct((lay.U, lay.pay, CH), BF16)],
        [HB] * 4,
        out_specs=[HB],
        scratch=[
            pltpu.VMEM((lay.U, lay.pay, CH), BF16),
            pltpu.VMEM(ingest_features.shape, BF16),
            pltpu.VMEM((8, CH), jnp.int32),
            pltpu.SMEM((1,), jnp.int32),
            pltpu.VMEM((1, lay.slots), jnp.int32),
            pltpu.VMEM(tile_ids.shape[::-1], jnp.int32),
            pltpu.SemaphoreType.DMA((4,)),
            pltpu.SemaphoreType.DMA((lay.U,)),
        ],
        vmem=PACK_VMEM,
    )(unit_rows, node_map.reshape(1, lay.slots), tile_ids.T, ingest_features)
    got = lax.all_to_all(outgoing, ("row", "col"), split_axis=0, concat_axis=0, tiled=True)

    _, token = call(seen_kernel, [], [VM], flops=SEEN_FLOPS)(val3[0])

    def land(first, many, token, extra=()):
        (x, *more), token = call(
            functools.partial(land_kernel, lay, first, many),
            [array(lay.own, many * CH), *extra],
            [VM],
            behind=[token],
        )(got)
        return [x] + [exchange(x, chip=s) for s in range(1, lay.chips)], more, token

    def dense(turned, token):
        depth = 2 * lay.chips * PIECE + TILE
        shape = (lay.chip_cols, depth) if turned else (depth, lay.chip_cols)
        return call(
            functools.partial(dense_kernel, lay, turned),
            [array(*shape)] * 2,
            [SM, HB, HB, VM, VM, VM, VM],
            behind=[token],
            scratch=[pltpu.VMEM(tile_values.shape, BF16)] * 2 + [pltpu.SemaphoreType.DMA((2,))],
        )(ids, *values)

    xs, (ids,), token = land(*GATHER[0], token, [array(8, CH, jnp.int32)])
    gathered = [xs]
    (at0, at1), token = dense(True, token)
    for first, many in GATHER[1:]:
        xs, _, token = land(first, many, token)
        gathered.append(xs)
    own = [xs[0] for xs in gathered]

    def back(n, token, wait=()):
        first, many = SUMS[n]
        where, lo = inside(GATHER, first, many)
        (mine,), token = call(
            functools.partial(back_kernel, lay.chips, lo, many * CH),
            [array(lay.chip_cols, many * CH)],
            [VM] * (2 + lay.chips),
            behind=[token, *wait],
            flops=0 if n else FIRST_FLOPS,
        )(at0, at1, *gathered[where])
        return [mine] + [exchange(mine, dl=s) for s in range(1, lay.R2)], token

    def forward(sums, token):
        shape = sums[0].shape
        (hidden, *sent), token = call(
            functools.partial(encode_kernel, lay.R2),
            [array(*shape)] + [array(lay.own, shape[1])] * (lay.chips - 1),
            [VM] * (3 + lay.R2),
            behind=[token],
        )(mix_in, *sums, a0, a1)
        kept, _ = call(
            functools.partial(forward_kernel, 0),
            [array(lay.own, shape[1])],
            [VM] * 3,
            behind=[token],
        )(a0, a1, hidden)
        return kept + [exchange(f, chip=s + 1) for s, f in enumerate(sent)], token

    def decode(n, parts, left, token, flops=0):
        first, many = SUMS[n]
        done = left[0].shape[1] if left else 0
        return call(
            functools.partial(decode_kernel, lay.chips, len(own), first * CH, done),
            [array(PIECE, done + many * CH, F32 if i == 0 else BF16) for i in range(4)],
            [VM] * (1 + len(own) + lay.chips + len(left)),
            behind=[token],
            flops=flops,
        )(mix_out, *own, *parts, *left)

    def deliver(left):
        return [
            left[0],
            exchange(left[1], core=1),
            exchange(left[2], dh=1),
            exchange(left[3], dh=1, core=1),
        ]

    left, parts = [], []
    ready, token = back(0, token)
    coming, token = back(1, token)
    (a0, a1), token = dense(False, token)
    for n in range(len(SUMS)):
        following = None
        if n + 2 < len(SUMS):
            following, token = back(n + 2, token, ready[1:])
        part, token = forward(ready, token)
        parts.append(part)
        if n > 0:
            left, token = decode(n - 1, parts[n - 1], left, token, DECODE_FLOPS)
        ready, coming = coming, following
    early = deliver(left)
    left, token = decode(len(SUMS) - 1, parts[-1], [], token)
    late = deliver(left)
    out = None
    for done, pieces in ((0, early), (early[0].shape[1], late)):
        width = pieces[0].shape[1]
        (out,), token = call(
            functools.partial(join_kernel if done else first_join_kernel, lay, done),
            [array(PIECE, QUARTERS * lay.qw, F32)],
            [HB] * (1 if done else 0) + [VM] * 4,
            behind=[token],
            flops=0 if done else SEEN_FLOPS,
            out_specs=[HB],
            scratch=[pltpu.VMEM((4, PIECE, width), F32), pltpu.SemaphoreType.DMA((4,))],
            aliases={0: 0} if done else None,
        )(*([out] if done else []), *pieces)
    return out


def solution(mesh):
    rows, cols = mesh.shape["row"], mesh.shape["col"]

    def run(ingest_features, node_map, *rest):
        VMEM_LIMIT[0] = (16 if rows * cols <= 32 else 56) * 1024 * 1024
        lay = Layout(
            rows, cols, node_map.shape[0] // (rows * cols), ingest_features.shape[1]
        )
        return jax.shard_map(
            functools.partial(local, lay),
            mesh=mesh,
            in_specs=(
                P(("row", "col"), None),
                P(("row", "col")),
                P(("row", "col")),
                P(("row", "col"), None),
                P(("row", "col"), None, None),
                P(),
                P(),
            ),
            out_specs=P(("row", "col"), None),
            check_vma=False,
        )(ingest_features, node_map, *rest)

    return run
```

```python
import functools

import jax
import jax.numpy as jnp
from jax import lax
from jax.experimental import pallas as pl
from jax.experimental.pallas import tpu as pltpu
from jax.sharding import PartitionSpec as P

CH = 128
TILE = 128
PIECE = 128
QUARTERS = 4
VMEM_LIMIT = [16 * 1024 * 1024]

epsilon = 1e-05

BF16 = jnp.bfloat16
F32 = jnp.float32
VM = pl.BlockSpec(memory_space=pltpu.VMEM)
SM = pl.BlockSpec(memory_space=pltpu.SMEM)
HB = pl.BlockSpec(memory_space=pltpu.HBM)


class Here:
    def __init__(self, lay):
        z, c = lax.axis_index("row"), lax.axis_index("col")
        self.col, self.unit = c, z * lay.C + c
        self.h, self.l = lay.split_z(z)
        self.chip, self.core = over(c, 2), rest(c, 2)
        self.quarter = self.h * 2 + self.core


def over(x, n):
    assert n & (n - 1) == 0
    return x >> (n.bit_length() - 1)


def rest(x, n):
    assert n & (n - 1) == 0
    return x & (n - 1)


def iota(shape, axis):
    return lax.broadcasted_iota(jnp.int32, shape, axis)


def call(kernel, out_shape, in_specs, behind=(), flops=0, scratch=(), vmem=None, out_specs=None, aliases=None):
    count, many = len(in_specs), len(out_shape)
    last = count + len(behind) + many

    def body(*refs):
        kernel(*refs[:count], *refs[count + len(behind) : last], *refs[last + 1 :])
        refs[last][...] = jnp.zeros_like(refs[last])

    run = pl.pallas_call(
        body,
        out_shape=list(out_shape) + [jax.ShapeDtypeStruct((8, CH), F32)],
        in_specs=list(in_specs) + [VM] * len(behind),
        out_specs=list(out_specs or [VM] * many) + [VM],
        input_output_aliases=aliases or {},
        scratch_shapes=list(scratch),
        compiler_params=pltpu.CompilerParams(vmem_limit_bytes=vmem or VMEM_LIMIT[0]),
        cost_estimate=pl.CostEstimate(flops=flops, bytes_accessed=0, transcendentals=0),
    )

    def apply(*args):
        *outs, token = run(*args, *behind)
        return outs, token

    return apply


def array(rows, columns, dtype=BF16):
    return jax.ShapeDtypeStruct((rows, columns), dtype)


class Layout:
    def __init__(self, rows, cols, slots, width):
        self.R, self.C = rows, cols
        self.R2, self.chips = rows // 2, cols // 2
        self.U = rows * cols
        self.slots = slots
        self.pair = slots // self.U
        self.slab = 4 * self.pair
        self.upl = CH // self.slab
        self.groups = width // CH // QUARTERS
        self.qw = self.groups * CH
        self.blocks = self.R2 * self.chips
        self.own = 4 * PIECE
        self.chip_cols = 2 * rows * TILE
        self.pay = self.groups * self.slab + 8

    def split_z(self, z):
        return rest(z, 2), over(z, 2)

    def join_z(self, h, l):
        return l * 2 + h


def pack_kernel(lay, held_far, node_far, tiles_far, feats_far, out_far, out, feats, ids, held, node, tiles, arrived, gone):
    unit = Here(lay).unit
    n = lay.slots
    pairs = ((held_far, held), (node_far, node), (tiles_far, tiles), (feats_far, feats))
    first = [pltpu.make_async_copy(a, b, arrived.at[i]) for i, (a, b) in enumerate(pairs)]
    for copy in first:
        copy.start()
    bring = first.pop()
    for copy in first:
        copy.wait()
    count = held[0]
    ids[...] = jnp.zeros_like(ids)
    ids[1:3, 0 : tiles.shape[1]] = tiles[...]
    row = node[...]
    slot = iota((1, n), 1)
    live = slot < count
    p = over(row, PIECE)
    h, l = lay.split_z(over(p, lay.C))
    c = rest(p, lay.C)
    block = l * lay.chips + over(c, 2)
    part = h * 2 + rest(c, 2)
    p = jnp.where(live, p, -1)
    across = jnp.broadcast_to(p, (n, n))
    down = jnp.transpose(across)
    before = (across == down) & (iota((n, n), 0) < iota((n, n), 1))
    rank = jnp.sum(jnp.where(before, 1, 0), axis=0, keepdims=True)
    target = jnp.where(live, (block * 4 + part) * lay.pair + rank, -1)
    pick = jnp.where(iota((n, n), 0) == target, 1.0, 0.0).astype(BF16)
    place = jnp.where(live, rest(row, PIECE) + 1, 0).astype(F32).astype(BF16)
    place = jnp.broadcast_to(place, (16, n))
    places = lax.dot_general(
        place, pick, (((1,), (1,)), ((), ())), preferred_element_type=F32
    )
    block = over(iota((lay.blocks, n), 1), lay.slab) == iota((lay.blocks, n), 0)
    place = jnp.where(block, places[0:1, :], 0.0).astype(BF16)
    fro, to = iota((n, CH), 0), iota((n, CH), 1)
    move = (rest(fro, lay.slab) == rest(to, lay.slab)) & (
        over(to, lay.slab) == rest(unit, lay.upl)
    )
    move = jnp.where(move, 1.0, 0.0).astype(BF16)
    places = jnp.dot(place, move, preferred_element_type=F32)
    top = iota((8, CH), 0) == 0
    lower = ids[...].astype(F32)
    bring.wait()
    below = [
        jnp.where(top, places[b : b + 1, :], lower).astype(BF16)
        for b in range(lay.blocks)
    ]
    for q in range(QUARTERS):
        ordered = jnp.dot(
            pick, feats[:, q * lay.qw : (q + 1) * lay.qw], preferred_element_type=F32
        ).astype(BF16)
        for l in range(lay.R2):
            for chip in range(lay.chips):
                b = l * lay.chips + chip
                d = lay.join_z(q // 2, l) * lay.C + chip * 2 + q % 2
                for g in range(lay.groups):
                    out[d, g * lay.slab : (g + 1) * lay.slab, :] = ordered[
                        b * lay.slab : (b + 1) * lay.slab, g * CH : (g + 1) * CH
                    ]
                out[d, lay.groups * lay.slab : lay.pay, :] = below[b]
    send = pltpu.make_async_copy(out, out_far, gone)
    send.start()
    send.wait()


def land_kernel(lay, first, many, got, out, ids=None):
    here = Here(lay)
    lane = iota((1, CH), 1)
    part = (lane % lay.slab) // lay.pair
    base = (part ^ here.quarter) * PIECE - 1
    rows = iota((lay.own, CH), 0)
    picks = []
    for j in range(lay.U // lay.upl):
        total = jnp.zeros((8, CH), F32)
        for i in range(lay.upl):
            total = total + got[j * lay.upl + i, lay.groups * lay.slab : lay.pay, :].astype(F32)
        place = total[0:1, :].astype(jnp.int32)
        spot = jnp.where(place > 0, base + place, -1)
        picks.append(jnp.where(rows == spot, 1.0, 0.0).astype(BF16))
    pick = jnp.concatenate(picks, axis=1)
    for g in range(many):
        lo = (first + g) * lay.slab
        block = got[:, lo : lo + lay.slab, :].reshape(lay.U * lay.slab, CH)
        out[:, g * CH : (g + 1) * CH] = jnp.dot(
            pick, block, preferred_element_type=F32
        ).astype(BF16)
    if ids is not None:
        for i in range(4):
            z = lay.join_z(here.h ^ (i % 2), here.l)
            found = got[z * lay.C + (here.col ^ (i // 2)), lay.groups * lay.slab : lay.pay, :].astype(F32)
            ids[2 * i : 2 * i + 2, :] = found[1:3, :].astype(jnp.int32)


def dense_kernel(lay, turned, *refs):
    here = Here(lay)
    far_ids, sources, (near, far, ids), held, arrived = refs[0], refs[1:7], refs[7:10], refs[10:16], refs[16]
    fetch = [
        pltpu.make_async_copy(src, dst, arrived.at[i])
        for i, (src, dst) in enumerate(zip((*sources, far_ids), (*held, ids)))
    ]
    for copy in fetch:
        copy.start()
    near[...] = jnp.zeros_like(near)
    far[...] = jnp.zeros_like(far)
    fetch[-1].wait()
    spare = 2 * lay.chips
    cut = held[2].shape[0]
    order = ((2, 1, 0, far), (4, 3, 0, far), (0, 0, 0, near), (1, 2, 0, near), (3, 1, cut, far), (5, 3, cut, far))
    for n, i, skip, to in order:
        values = held[n]
        fetch[n].wait()

        def body(t, carry, i=i, skip=skip, values=values, to=to):
            rt, ct = ids[2 * i, skip + t], ids[2 * i + 1, skip + t]
            c = rest(rt, lay.C)
            r = (over(c, 2) ^ here.chip) * 2 + (rest(c, 2) ^ here.core)
            k = rest(over(ct, lay.R), 2) * lay.R + rest(ct, lay.R)
            r = jnp.where(rt < lay.U, r, spare)
            rr = pl.ds(pl.multiple_of(r * TILE, TILE), TILE)
            kk = pl.ds(pl.multiple_of(k * TILE, TILE), TILE)
            if turned:
                to[kk, rr] = jnp.transpose(values[t])
            else:
                to[rr, kk] = values[t]
            return carry

        lax.fori_loop(0, values.shape[0], body, 0, unroll=min(4, values.shape[0]))


def seen_kernel(*refs):
    pass


def back_kernel(chips, lo, width, *refs):
    at0, at1, xs, out = refs[0], refs[1], refs[2 : 2 + chips], refs[2 + chips]
    span = slice(lo, lo + width)
    near = jnp.concatenate([x[0 : 2 * PIECE, span] for x in xs], axis=0)
    depth = near.shape[0]
    far = jnp.concatenate([x[2 * PIECE : 4 * PIECE, span] for x in xs], axis=0)
    for lo in range(0, out.shape[0], BLOCK):
        rows = slice(lo, lo + BLOCK)
        total = jnp.dot(at0[rows, 0:depth], near, preferred_element_type=F32)
        total += jnp.dot(at1[rows, 0:depth], far, preferred_element_type=F32)
        out[rows, :] = total.astype(BF16)


def forward_kernel(first, a0, a1, hidden, *outs):
    for i, out in enumerate(outs):
        rows = slice((first + i) * 2 * PIECE, (first + i + 1) * 2 * PIECE)
        for lo, a in ((0, a0), (2 * PIECE, a1)):
            total = jnp.dot(a[rows, :], hidden[...], preferred_element_type=F32)
            out[lo : lo + 2 * PIECE, :] = total.astype(BF16)


def unit_groups(total):
    power = jnp.mean(total * total, axis=-1, keepdims=True)
    return (total * lax.rsqrt(power + epsilon)).astype(BF16)


def encode_kernel(parts, mix, *refs):
    sums, a0, a1, hidden, outs = refs[:parts], refs[parts], refs[parts + 1], refs[parts + 2], refs[parts + 3 :]
    for g in range(hidden.shape[1] // CH):
        span = slice(g * CH, (g + 1) * CH)
        total = sums[0][:, span].astype(F32)
        for ref in sums[1:]:
            total = total + ref[:, span].astype(F32)
        v = jnp.dot(unit_groups(total), mix[...], preferred_element_type=F32)
        hidden[:, span] = (0.5 * v * (1.0 + lax.erf(v * (0.5**0.5)))).astype(BF16)
    forward_kernel(1, a0, a1, hidden, *outs)


def decode_kernel(parts, takes, lo, done, mix, *refs):
    xs, totals = refs[:takes], refs[takes : takes + parts]
    early, outs = refs[takes + parts : -4], refs[-4:]
    for out, ref in zip(outs, early):
        out[:, 0:done] = ref[...]
    x_at = [(x, at) for x in xs for at in range(0, x.shape[1], CH)][lo // CH :]
    for g in range(totals[0].shape[1] // CH):
        span = slice(g * CH, (g + 1) * CH)
        total = totals[0][:, span].astype(F32)
        for ref in totals[1:]:
            total = total + ref[:, span].astype(F32)
        recon = jnp.dot(unit_groups(total), mix[...], preferred_element_type=F32)
        x, at = x_at[g]
        left = x[:, at : at + CH].astype(F32) - recon
        for i, out in enumerate(outs):
            to = slice(done + g * CH, done + (g + 1) * CH)
            out[:, to] = left[i * PIECE : (i + 1) * PIECE, :].astype(out.dtype)


def join_kernel(lay, done, kept, *refs):
    pieces = refs[:4]
    far, wide, gone = refs[-3:]
    mine, width = Here(lay).quarter, pieces[0].shape[1]
    copies = []
    for rel, ref in enumerate(pieces):
        wide[rel] = ref[...].astype(F32)
        at = pl.multiple_of((mine ^ rel) * lay.qw + done, CH)
        copies.append(
            pltpu.make_async_copy(wide.at[rel], far.at[:, pl.ds(at, width)], gone.at[rel])
        )
        copies[-1].start()
    for copy in copies:
        copy.wait()


def first_join_kernel(lay, done, *refs):
    join_kernel(lay, done, None, *refs)


GATHER = ((0, 1), (1, 1), (2, 1))
RELAY = False
SUMS = ((0, 1), (1, 1), (2, 1))
BLOCK = 256
AHEAD = 5
PACK_VMEM = 58 * 1024 * 1024
SEEN_FLOPS = 7_500_000_000
FIRST_FLOPS = 5_000_000_000
DECODE_FLOPS = 3_000_000_000


def inside(parts, first, many):
    for n, (f, m) in enumerate(parts):
        if f <= first and first + many <= f + m:
            return n, (first - f) * CH
    raise ValueError("not nested")


def local(lay, ingest_features, node_map, unit_rows, tile_ids, tile_values, mix_in, mix_out):
    def exchange(x, dh=0, dl=0, chip=0, core=0):
        pairs = []
        for zz in range(lay.R):
            hh, ll = lay.split_z(zz)
            for cc in range(lay.C):
                to = lay.join_z(hh ^ dh, ll ^ dl) * lay.C + (cc ^ (chip * 2 + core))
                pairs.append((zz * lay.C + cc, to))
        return lax.ppermute(x, ("row", "col"), pairs)

    cut = tile_values.shape[0] * AHEAD // 8
    val1 = [exchange(x, dh=1) for x in (tile_values[:cut], tile_values[cut:])]
    val2 = exchange(tile_values, core=1)
    val3 = [exchange(x, core=1) for x in val1]
    values = (tile_values, val2, *val1, *val3)

    (outgoing,), _ = call(
        functools.partial(pack_kernel, lay),
        [jax.ShapeDtypeStruct((lay.U, lay.pay, CH), BF16)],
        [HB] * 4,
        out_specs=[HB],
        scratch=[
            pltpu.VMEM((lay.U, lay.pay, CH), BF16),
            pltpu.VMEM(ingest_features.shape, BF16),
            pltpu.VMEM((8, CH), jnp.int32),
            pltpu.SMEM((1,), jnp.int32),
            pltpu.VMEM((1, lay.slots), jnp.int32),
            pltpu.VMEM(tile_ids.shape[::-1], jnp.int32),
            pltpu.SemaphoreType.DMA((4,)),
            pltpu.SemaphoreType.DMA(()),
        ],
        vmem=PACK_VMEM,
    )(unit_rows, node_map.reshape(1, lay.slots), tile_ids.T, ingest_features)
    got = lax.all_to_all(outgoing, ("row", "col"), split_axis=0, concat_axis=0, tiled=True)

    _, token = call(seen_kernel, [], [VM], flops=SEEN_FLOPS)(val3[0])

    def land(first, many, token, extra=(), relay=False):
        (x, *more), token = call(
            functools.partial(land_kernel, lay, first, many),
            [array(lay.own, many * CH), *extra],
            [VM],
            behind=[token],
        )(got)
        if relay:
            xs = [x]
            while len(xs) < lay.chips:
                xs += [exchange(y, chip=len(xs)) for y in list(xs)]
        else:
            xs = [x] + [exchange(x, chip=s) for s in range(1, lay.chips)]
        return xs, more, token

    def dense(turned, token):
        depth = 2 * lay.chips * PIECE + TILE
        shape = (lay.chip_cols, depth) if turned else (depth, lay.chip_cols)
        return call(
            functools.partial(dense_kernel, lay, turned),
            [array(*shape)] * 2,
            [HB] * 7,
            behind=[token],
            scratch=[pltpu.SMEM((8, CH), jnp.int32)]
            + [pltpu.VMEM(x.shape, BF16) for x in values]
            + [pltpu.SemaphoreType.DMA((7,))],
        )(ids, *values)

    xs, (ids,), token = land(*GATHER[0], token, [array(8, CH, jnp.int32)])
    gathered = [xs]
    (at0, at1), token = dense(True, token)
    xs, _, token = land(*GATHER[1], token, relay=True)
    gathered.append(xs)

    def back(n, token, wait=()):
        first, many = SUMS[n]
        where, lo = inside(GATHER, first, many)
        (mine,), token = call(
            functools.partial(back_kernel, lay.chips, lo, many * CH),
            [array(lay.chip_cols, many * CH)],
            [VM] * (2 + lay.chips),
            behind=[token, *wait],
            flops=0 if n else FIRST_FLOPS,
        )(at0, at1, *gathered[where])
        return [mine] + [exchange(mine, dl=s) for s in range(1, lay.R2)], token

    def forward(sums, token):
        shape = sums[0].shape
        (hidden, *sent), token = call(
            functools.partial(encode_kernel, lay.R2),
            [array(*shape)] + [array(lay.own, shape[1])] * (lay.chips - 1),
            [VM] * (3 + lay.R2),
            behind=[token],
        )(mix_in, *sums, a0, a1)
        kept, _ = call(
            functools.partial(forward_kernel, 0),
            [array(lay.own, shape[1])],
            [VM] * 3,
            behind=[token],
        )(a0, a1, hidden)
        return kept + [exchange(f, chip=s + 1) for s, f in enumerate(sent)], token

    def decode(n, parts, left, token, flops=0):
        first, many = SUMS[n]
        done = left[0].shape[1] if left else 0
        return call(
            functools.partial(decode_kernel, lay.chips, len(own), first * CH, done),
            [array(PIECE, done + many * CH, F32 if i == 0 else BF16) for i in range(4)],
            [VM] * (1 + len(own) + lay.chips + len(left)),
            behind=[token],
            flops=flops,
        )(mix_out, *own, *parts, *left)

    def deliver(left):
        return [
            left[0],
            exchange(left[1], core=1),
            exchange(left[2], dh=1),
            exchange(left[3], dh=1, core=1),
        ]

    left, parts = [], []
    ready, token = back(0, token)
    for first, many in GATHER[2:]:
        xs, _, token = land(first, many, token, relay=RELAY)
        gathered.append(xs)
    own = [xs[0] for xs in gathered]
    coming, token = back(1, token)
    (a0, a1), token = dense(False, token)
    for n in range(len(SUMS)):
        following = None
        if n + 2 < len(SUMS):
            following, token = back(n + 2, token, ready[1:])
        part, token = forward(ready, token)
        parts.append(part)
        if n > 0:
            left, token = decode(n - 1, parts[n - 1], left, token, DECODE_FLOPS)
        ready, coming = coming, following
    early = deliver(left)
    left, token = decode(len(SUMS) - 1, parts[-1], [], token)
    late = deliver(left)
    out = None
    for done, pieces in ((0, early), (early[0].shape[1], late)):
        width = pieces[0].shape[1]
        (out,), token = call(
            functools.partial(join_kernel if done else first_join_kernel, lay, done),
            [array(PIECE, QUARTERS * lay.qw, F32)],
            [HB] * (1 if done else 0) + [VM] * 4,
            behind=[token],
            flops=0 if done else SEEN_FLOPS,
            out_specs=[HB],
            scratch=[pltpu.VMEM((4, PIECE, width), F32), pltpu.SemaphoreType.DMA((4,))],
            aliases={0: 0} if done else None,
        )(*([out] if done else []), *pieces)
    return out


def solution(mesh):
    rows, cols = mesh.shape["row"], mesh.shape["col"]

    def run(ingest_features, node_map, *rest):
        VMEM_LIMIT[0] = (16 if rows * cols <= 32 else 56) * 1024 * 1024
        lay = Layout(
            rows, cols, node_map.shape[0] // (rows * cols), ingest_features.shape[1]
        )
        return jax.shard_map(
            functools.partial(local, lay),
            mesh=mesh,
            in_specs=(
                P(("row", "col"), None),
                P(("row", "col")),
                P(("row", "col")),
                P(("row", "col"), None),
                P(("row", "col"), None, None),
                P(),
                P(),
            ),
            out_specs=P(("row", "col"), None),
            check_vma=False,
        )(ingest_features, node_map, *rest)

    return run
```

```python
import functools

import jax
import jax.numpy as jnp
from jax import lax
from jax.experimental import pallas as pl
from jax.experimental.pallas import tpu as pltpu
from jax.sharding import PartitionSpec as P

CH = 128
TILE = 128
PIECE = 128
QUARTERS = 4
VMEM_LIMIT = [16 * 1024 * 1024]

epsilon = 1e-05

BF16 = jnp.bfloat16
F32 = jnp.float32
VM = pl.BlockSpec(memory_space=pltpu.VMEM)
SM = pl.BlockSpec(memory_space=pltpu.SMEM)
HB = pl.BlockSpec(memory_space=pltpu.HBM)


class Here:
    def __init__(self, lay):
        z, c = lax.axis_index("row"), lax.axis_index("col")
        self.col, self.unit = c, z * lay.C + c
        self.h, self.l = lay.split_z(z)
        self.chip, self.core = over(c, 2), rest(c, 2)
        self.quarter = self.h * 2 + self.core


def over(x, n):
    assert n & (n - 1) == 0
    return x >> (n.bit_length() - 1)


def rest(x, n):
    assert n & (n - 1) == 0
    return x & (n - 1)


def iota(shape, axis):
    return lax.broadcasted_iota(jnp.int32, shape, axis)


def call(kernel, out_shape, in_specs, behind=(), flops=0, scratch=(), vmem=None, out_specs=None, aliases=None):
    count, many = len(in_specs), len(out_shape)
    last = count + len(behind) + many

    def body(*refs):
        kernel(*refs[:count], *refs[count + len(behind) : last], *refs[last + 1 :])
        refs[last][...] = jnp.zeros_like(refs[last])

    run = pl.pallas_call(
        body,
        out_shape=list(out_shape) + [jax.ShapeDtypeStruct((8, CH), F32)],
        in_specs=list(in_specs) + [VM] * len(behind),
        out_specs=list(out_specs or [VM] * many) + [VM],
        input_output_aliases=aliases or {},
        scratch_shapes=list(scratch),
        compiler_params=pltpu.CompilerParams(vmem_limit_bytes=vmem or VMEM_LIMIT[0]),
        cost_estimate=pl.CostEstimate(flops=flops, bytes_accessed=0, transcendentals=0),
    )

    def apply(*args):
        *outs, token = run(*args, *behind)
        return outs, token

    return apply


def array(rows, columns, dtype=BF16):
    return jax.ShapeDtypeStruct((rows, columns), dtype)


class Layout:
    def __init__(self, rows, cols, slots, width):
        self.R, self.C = rows, cols
        self.R2, self.chips = rows // 2, cols // 2
        self.U = rows * cols
        self.slots = slots
        self.pair = slots // self.U
        self.slab = 4 * self.pair
        self.upl = CH // self.slab
        self.groups = width // CH // QUARTERS
        self.qw = self.groups * CH
        self.blocks = self.R2 * self.chips
        self.own = 4 * PIECE
        self.chip_cols = 2 * rows * TILE
        self.pay = self.groups * self.slab + 8

    def split_z(self, z):
        return rest(z, 2), over(z, 2)

    def join_z(self, h, l):
        return l * 2 + h


def pack_kernel(lay, held_far, node_far, tiles_far, feats_far, out_far, out, feats, ids, held, node, tiles, arrived, gone):
    unit = Here(lay).unit
    n = lay.slots
    pairs = ((held_far, held), (node_far, node), (tiles_far, tiles), (feats_far, feats))
    first = [pltpu.make_async_copy(a, b, arrived.at[i]) for i, (a, b) in enumerate(pairs)]
    for copy in first:
        copy.start()
    bring = first.pop()
    for copy in first:
        copy.wait()
    count = held[0]
    ids[...] = jnp.zeros_like(ids)
    ids[1:3, 0 : tiles.shape[1]] = tiles[...]
    row = node[...]
    slot = iota((1, n), 1)
    live = slot < count
    p = over(row, PIECE)
    h, l = lay.split_z(over(p, lay.C))
    c = rest(p, lay.C)
    block = l * lay.chips + over(c, 2)
    part = h * 2 + rest(c, 2)
    p = jnp.where(live, p, -1)
    across = jnp.broadcast_to(p, (n, n))
    down = jnp.transpose(across)
    before = (across == down) & (iota((n, n), 0) < iota((n, n), 1))
    rank = jnp.sum(jnp.where(before, 1, 0), axis=0, keepdims=True)
    target = jnp.where(live, (block * 4 + part) * lay.pair + rank, -1)
    pick = jnp.where(iota((n, n), 0) == target, 1.0, 0.0).astype(BF16)
    place = jnp.where(live, rest(row, PIECE) + 1, 0).astype(F32).astype(BF16)
    place = jnp.broadcast_to(place, (16, n))
    places = lax.dot_general(
        place, pick, (((1,), (1,)), ((), ())), preferred_element_type=F32
    )
    block = over(iota((lay.blocks, n), 1), lay.slab) == iota((lay.blocks, n), 0)
    place = jnp.where(block, places[0:1, :], 0.0).astype(BF16)
    fro, to = iota((n, CH), 0), iota((n, CH), 1)
    move = (rest(fro, lay.slab) == rest(to, lay.slab)) & (
        over(to, lay.slab) == rest(unit, lay.upl)
    )
    move = jnp.where(move, 1.0, 0.0).astype(BF16)
    places = jnp.dot(place, move, preferred_element_type=F32)
    top = iota((8, CH), 0) == 0
    lower = ids[...].astype(F32)
    bring.wait()
    below = [
        jnp.where(top, places[b : b + 1, :], lower).astype(BF16)
        for b in range(lay.blocks)
    ]
    for q in range(QUARTERS):
        ordered = jnp.dot(
            pick, feats[:, q * lay.qw : (q + 1) * lay.qw], preferred_element_type=F32
        ).astype(BF16)
        for l in range(lay.R2):
            for chip in range(lay.chips):
                b = l * lay.chips + chip
                d = lay.join_z(q // 2, l) * lay.C + chip * 2 + q % 2
                for g in range(lay.groups):
                    out[d, g * lay.slab : (g + 1) * lay.slab, :] = ordered[
                        b * lay.slab : (b + 1) * lay.slab, g * CH : (g + 1) * CH
                    ]
                out[d, lay.groups * lay.slab : lay.pay, :] = below[b]
    send = pltpu.make_async_copy(out, out_far, gone)
    send.start()
    send.wait()


def land_kernel(lay, first, many, got, out, ids=None):
    here = Here(lay)
    lane = iota((1, CH), 1)
    part = (lane % lay.slab) // lay.pair
    base = (part ^ here.quarter) * PIECE - 1
    rows = iota((lay.own, CH), 0)
    picks = []
    for j in range(lay.U // lay.upl):
        total = jnp.zeros((8, CH), F32)
        for i in range(lay.upl):
            total = total + got[j * lay.upl + i, lay.groups * lay.slab : lay.pay, :].astype(F32)
        place = total[0:1, :].astype(jnp.int32)
        spot = jnp.where(place > 0, base + place, -1)
        picks.append(jnp.where(rows == spot, 1.0, 0.0).astype(BF16))
    pick = jnp.concatenate(picks, axis=1)
    for g in range(many):
        lo = (first + g) * lay.slab
        block = got[:, lo : lo + lay.slab, :].reshape(lay.U * lay.slab, CH)
        out[:, g * CH : (g + 1) * CH] = jnp.dot(
            pick, block, preferred_element_type=F32
        ).astype(BF16)
    if ids is not None:
        for i in range(4):
            z = lay.join_z(here.h ^ (i % 2), here.l)
            found = got[z * lay.C + (here.col ^ (i // 2)), lay.groups * lay.slab : lay.pay, :].astype(F32)
            ids[2 * i : 2 * i + 2, :] = found[1:3, :].astype(jnp.int32)


def dense_kernel(lay, turned, *refs):
    here = Here(lay)
    far_ids, sources, (near, far, ids), held, arrived = refs[0], refs[1:7], refs[7:10], refs[10:16], refs[16]
    fetch = [
        pltpu.make_async_copy(src, dst, arrived.at[i])
        for i, (src, dst) in enumerate(zip((*sources, far_ids), (*held, ids)))
    ]
    for copy in fetch:
        copy.start()
    near[...] = jnp.zeros_like(near)
    far[...] = jnp.zeros_like(far)
    fetch[-1].wait()
    spare = 2 * lay.chips
    cut = held[2].shape[0]
    order = ((2, 1, 0, far), (4, 3, 0, far), (0, 0, 0, near), (1, 2, 0, near), (3, 1, cut, far), (5, 3, cut, far))
    for n, i, skip, to in order:
        values = held[n]
        fetch[n].wait()

        def body(t, carry, i=i, skip=skip, values=values, to=to):
            rt, ct = ids[2 * i, skip + t], ids[2 * i + 1, skip + t]
            c = rest(rt, lay.C)
            r = (over(c, 2) ^ here.chip) * 2 + (rest(c, 2) ^ here.core)
            k = rest(over(ct, lay.R), 2) * lay.R + rest(ct, lay.R)
            r = jnp.where(rt < lay.U, r, spare)
            rr = pl.ds(pl.multiple_of(r * TILE, TILE), TILE)
            kk = pl.ds(pl.multiple_of(k * TILE, TILE), TILE)
            if turned:
                to[kk, rr] = jnp.transpose(values[t])
            else:
                to[rr, kk] = values[t]
            return carry

        lax.fori_loop(0, values.shape[0], body, 0, unroll=min(4, values.shape[0]))


def seen_kernel(*refs):
    pass


def back_kernel(chips, lo, width, *refs):
    at0, at1, xs, out = refs[0], refs[1], refs[2 : 2 + chips], refs[2 + chips]
    span = slice(lo, lo + width)
    near = jnp.concatenate([x[0 : 2 * PIECE, span] for x in xs], axis=0)
    depth = near.shape[0]
    far = jnp.concatenate([x[2 * PIECE : 4 * PIECE, span] for x in xs], axis=0)
    for lo in range(0, out.shape[0], BLOCK):
        rows = slice(lo, lo + BLOCK)
        total = jnp.dot(at0[rows, 0:depth], near, preferred_element_type=F32)
        total += jnp.dot(at1[rows, 0:depth], far, preferred_element_type=F32)
        out[rows, :] = total.astype(BF16)


def forward_kernel(first, a0, a1, hidden, *outs):
    for i, out in enumerate(outs):
        rows = slice((first + i) * 2 * PIECE, (first + i + 1) * 2 * PIECE)
        for lo, a in ((0, a0), (2 * PIECE, a1)):
            total = jnp.dot(a[rows, :], hidden[...], preferred_element_type=F32)
            out[lo : lo + 2 * PIECE, :] = total.astype(BF16)


def unit_groups(total):
    power = jnp.mean(total * total, axis=-1, keepdims=True)
    return (total * lax.rsqrt(power + epsilon)).astype(BF16)


def encode_kernel(parts, mix, *refs):
    sums, a0, a1, hidden, outs = refs[:parts], refs[parts], refs[parts + 1], refs[parts + 2], refs[parts + 3 :]
    for g in range(hidden.shape[1] // CH):
        span = slice(g * CH, (g + 1) * CH)
        total = sums[0][:, span].astype(F32)
        for ref in sums[1:]:
            total = total + ref[:, span].astype(F32)
        v = jnp.dot(unit_groups(total), mix[...], preferred_element_type=F32)
        hidden[:, span] = (0.5 * v * (1.0 + lax.erf(v * (0.5**0.5)))).astype(BF16)
    forward_kernel(1, a0, a1, hidden, *outs)


def decode_kernel(parts, takes, lo, done, mix, *refs):
    xs, totals = refs[:takes], refs[takes : takes + parts]
    early, outs = refs[takes + parts : -4], refs[-4:]
    for out, ref in zip(outs, early):
        out[:, 0:done] = ref[...]
    x_at = [(x, at) for x in xs for at in range(0, x.shape[1], CH)][lo // CH :]
    for g in range(totals[0].shape[1] // CH):
        span = slice(g * CH, (g + 1) * CH)
        total = totals[0][:, span].astype(F32)
        for ref in totals[1:]:
            total = total + ref[:, span].astype(F32)
        recon = jnp.dot(unit_groups(total), mix[...], preferred_element_type=F32)
        x, at = x_at[g]
        left = x[:, at : at + CH].astype(F32) - recon
        for i, out in enumerate(outs):
            to = slice(done + g * CH, done + (g + 1) * CH)
            out[:, to] = left[i * PIECE : (i + 1) * PIECE, :].astype(out.dtype)


def join_kernel(lay, done, kept, *refs):
    pieces = refs[:4]
    far, wide, gone = refs[-3:]
    mine, width = Here(lay).quarter, pieces[0].shape[1]
    copies = []
    for rel, ref in enumerate(pieces):
        wide[rel] = ref[...].astype(F32)
        at = pl.multiple_of((mine ^ rel) * lay.qw + done, CH)
        copies.append(
            pltpu.make_async_copy(wide.at[rel], far.at[:, pl.ds(at, width)], gone.at[rel])
        )
        copies[-1].start()
    for copy in copies:
        copy.wait()


def first_join_kernel(lay, done, *refs):
    join_kernel(lay, done, None, *refs)


GATHER = ((0, 1), (1, 1), (2, 1))
RELAY = False
SUMS = ((0, 1), (1, 1), (2, 1))
BLOCK = 256
AHEAD = 16
PACK_VMEM = 58 * 1024 * 1024
SEEN_FLOPS = 7_500_000_000
FIRST_FLOPS = 5_000_000_000
DECODE_FLOPS = 3_000_000_000


def inside(parts, first, many):
    for n, (f, m) in enumerate(parts):
        if f <= first and first + many <= f + m:
            return n, (first - f) * CH
    raise ValueError("not nested")


def local(lay, ingest_features, node_map, unit_rows, tile_ids, tile_values, mix_in, mix_out):
    def exchange(x, dh=0, dl=0, chip=0, core=0):
        pairs = []
        for zz in range(lay.R):
            hh, ll = lay.split_z(zz)
            for cc in range(lay.C):
                to = lay.join_z(hh ^ dh, ll ^ dl) * lay.C + (cc ^ (chip * 2 + core))
                pairs.append((zz * lay.C + cc, to))
        return lax.ppermute(x, ("row", "col"), pairs)

    cut = tile_values.shape[0] * AHEAD // 24
    val1 = [exchange(x, dh=1) for x in (tile_values[:cut], tile_values[cut:])]
    val2 = exchange(tile_values, core=1)
    val3 = [exchange(x, core=1) for x in val1]
    values = (tile_values, val2, *val1, *val3)

    (outgoing,), _ = call(
        functools.partial(pack_kernel, lay),
        [jax.ShapeDtypeStruct((lay.U, lay.pay, CH), BF16)],
        [HB] * 4,
        out_specs=[HB],
        scratch=[
            pltpu.VMEM((lay.U, lay.pay, CH), BF16),
            pltpu.VMEM(ingest_features.shape, BF16),
            pltpu.VMEM((8, CH), jnp.int32),
            pltpu.SMEM((1,), jnp.int32),
            pltpu.VMEM((1, lay.slots), jnp.int32),
            pltpu.VMEM(tile_ids.shape[::-1], jnp.int32),
            pltpu.SemaphoreType.DMA((4,)),
            pltpu.SemaphoreType.DMA(()),
        ],
        vmem=PACK_VMEM,
    )(unit_rows, node_map.reshape(1, lay.slots), tile_ids.T, ingest_features)
    got = lax.all_to_all(outgoing, ("row", "col"), split_axis=0, concat_axis=0, tiled=True)

    _, token = call(seen_kernel, [], [VM], flops=SEEN_FLOPS)(val3[0])

    def land(first, many, token, extra=(), relay=False):
        (x, *more), token = call(
            functools.partial(land_kernel, lay, first, many),
            [array(lay.own, many * CH), *extra],
            [VM],
            behind=[token],
        )(got)
        if relay:
            xs = [x]
            while len(xs) < lay.chips:
                xs += [exchange(y, chip=len(xs)) for y in list(xs)]
        else:
            xs = [x] + [exchange(x, chip=s) for s in range(1, lay.chips)]
        return xs, more, token

    def dense(turned, token):
        depth = 2 * lay.chips * PIECE + TILE
        shape = (lay.chip_cols, depth) if turned else (depth, lay.chip_cols)
        return call(
            functools.partial(dense_kernel, lay, turned),
            [array(*shape)] * 2,
            [HB] * 7,
            behind=[token],
            scratch=[pltpu.SMEM((8, CH), jnp.int32)]
            + [pltpu.VMEM(x.shape, BF16) for x in values]
            + [pltpu.SemaphoreType.DMA((7,))],
        )(ids, *values)

    xs, (ids,), token = land(*GATHER[0], token, [array(8, CH, jnp.int32)])
    gathered = [xs]
    (at0, at1), token = dense(True, token)
    xs, _, token = land(*GATHER[1], token, relay=True)
    gathered.append(xs)

    def back(n, token, wait=()):
        first, many = SUMS[n]
        where, lo = inside(GATHER, first, many)
        (mine,), token = call(
            functools.partial(back_kernel, lay.chips, lo, many * CH),
            [array(lay.chip_cols, many * CH)],
            [VM] * (2 + lay.chips),
            behind=[token, *wait],
            flops=0 if n else FIRST_FLOPS,
        )(at0, at1, *gathered[where])
        return [mine] + [exchange(mine, dl=s) for s in range(1, lay.R2)], token

    def forward(sums, token):
        shape = sums[0].shape
        (hidden, *sent), token = call(
            functools.partial(encode_kernel, lay.R2),
            [array(*shape)] + [array(lay.own, shape[1])] * (lay.chips - 1),
            [VM] * (3 + lay.R2),
            behind=[token],
        )(mix_in, *sums, a0, a1)
        kept, _ = call(
            functools.partial(forward_kernel, 0),
            [array(lay.own, shape[1])],
            [VM] * 3,
            behind=[token],
        )(a0, a1, hidden)
        return kept + [exchange(f, chip=s + 1) for s, f in enumerate(sent)], token

    def decode(n, parts, left, token, flops=0):
        first, many = SUMS[n]
        done = left[0].shape[1] if left else 0
        return call(
            functools.partial(decode_kernel, lay.chips, len(own), first * CH, done),
            [array(PIECE, done + many * CH, F32 if i == 0 else BF16) for i in range(4)],
            [VM] * (1 + len(own) + lay.chips + len(left)),
            behind=[token],
            flops=flops,
        )(mix_out, *own, *parts, *left)

    def deliver(left):
        return [
            left[0],
            exchange(left[1], core=1),
            exchange(left[2], dh=1),
            exchange(left[3], dh=1, core=1),
        ]

    left, parts = [], []
    ready, token = back(0, token)
    for first, many in GATHER[2:]:
        xs, _, token = land(first, many, token, relay=RELAY)
        gathered.append(xs)
    own = [xs[0] for xs in gathered]
    coming, token = back(1, token)
    (a0, a1), token = dense(False, token)
    for n in range(len(SUMS)):
        following = None
        if n + 2 < len(SUMS):
            following, token = back(n + 2, token, ready[1:])
        part, token = forward(ready, token)
        parts.append(part)
        if n > 0:
            left, token = decode(n - 1, parts[n - 1], left, token, DECODE_FLOPS)
        ready, coming = coming, following
    early = deliver(left)
    left, token = decode(len(SUMS) - 1, parts[-1], [], token)
    late = deliver(left)
    out = None
    for done, pieces in ((0, early), (early[0].shape[1], late)):
        width = pieces[0].shape[1]
        (out,), token = call(
            functools.partial(join_kernel if done else first_join_kernel, lay, done),
            [array(PIECE, QUARTERS * lay.qw, F32)],
            [HB] * (1 if done else 0) + [VM] * 4,
            behind=[token],
            flops=0 if done else SEEN_FLOPS,
            out_specs=[HB],
            scratch=[pltpu.VMEM((4, PIECE, width), F32), pltpu.SemaphoreType.DMA((4,))],
            aliases={0: 0} if done else None,
        )(*([out] if done else []), *pieces)
    return out


def solution(mesh):
    rows, cols = mesh.shape["row"], mesh.shape["col"]

    def run(ingest_features, node_map, *rest):
        VMEM_LIMIT[0] = (16 if rows * cols <= 32 else 56) * 1024 * 1024
        lay = Layout(
            rows, cols, node_map.shape[0] // (rows * cols), ingest_features.shape[1]
        )
        return jax.shard_map(
            functools.partial(local, lay),
            mesh=mesh,
            in_specs=(
                P(("row", "col"), None),
                P(("row", "col")),
                P(("row", "col")),
                P(("row", "col"), None),
                P(("row", "col"), None, None),
                P(),
                P(),
            ),
            out_specs=P(("row", "col"), None),
            check_vma=False,
        )(ingest_features, node_map, *rest)

    return run
```
